32 devices in a mesh: section: 2 (over core), tensor: 4 (over z), dp: 4 (over y, x).
Axes of the slice: x: 2, y: 2, z: 4, core: 2. Of those that a mesh axis runs over, the one named last changes fastest.
Arguments:
- layer_input: bfloat16 [2, 1024, 1536], P(None, 'dp'), may hold values from -6 to 6
- seq_lengths: int32 [2, 4], replicated, may hold values from 1 to 896, 1024 in all within a row
- norm1_gain: float32 [2, 1536], P('section'), may hold values from 0.1 to 1.9
- w_query: bfloat16 [2, 1536, 1536], P('section', None, 'tensor'), may hold values from -0.15625 to 0.15625
- w_key: bfloat16 [2, 1536, 768], P('section', None, 'tensor'), may hold values from -0.15625 to 0.15625
- w_value: bfloat16 [2, 1536, 768], P('section', None, 'tensor'), may hold values from -0.15625 to 0.15625
- w_out: bfloat16 [2, 1536, 1536], P('section', 'tensor'), may hold values from -1 to 1
- norm2_gain: float32 [2, 1536], P('section'), may hold values from 0.1 to 1.9
- w_gate: bfloat16 [2, 1536, 4096], P('section', None, 'tensor'), may hold values from -0.15625 to 0.15625
- w_up: bfloat16 [2, 1536, 4096], P('section', None, 'tensor'), may hold values from -0.15625 to 0.15625
- w_down: bfloat16 [2, 4096, 1536], P('section', 'tensor'), may hold values from -0.09375 to 0.09375
- out_grad: bfloat16 [2, 1024, 1536], P(None, 'dp'), may hold values from -6 to 6
Outputs:
- activations: bfloat16 [2, 2, 1024, 1536], P('section', None, 'dp')
- input_grads: bfloat16 [2, 2, 1024, 1536], P('section', None, 'dp')
- grad_norm1: float32 [2, 1536], P('section', 'dp')
- grad_query: float32 [2, 1536, 1536], P('section', 'dp', 'tensor')
- grad_key: float32 [2, 1536, 768], P('section', 'dp', 'tensor')
- grad_value: float32 [2, 1536, 768], P('section', 'dp', 'tensor')
- grad_out: float32 [2, 1536, 1536], P('section', 'tensor', 'dp')
- grad_norm2: float32 [2, 1536], P('section', 'dp')
- grad_gate: float32 [2, 1536, 4096], P('section', 'dp', 'tensor')
- grad_up: float32 [2, 1536, 4096], P('section', 'dp', 'tensor')
- grad_down: float32 [2, 4096, 1536], P('section', 'tensor', 'dp')
The draws below stay inside these ranges and needn't reach their ends.
Inputs may be any that keep to these rules, and one draw needn't show every extreme that they name: `seq_lengths`: each row holds the lengths of the 4 sequences packed in order into one micro-batch; they sum to 1024, and the largest is exactly 896.
All inputs are finite; a program needn't handle non-finite values.
Results may differ from the reference program's by a relative error of at most 0.034.
Values may be sent and summed in bfloat16 or wider, within the bound.
No kernel may reach another device: no remote copies, remote signals or barrier semaphores. Data moves between devices by JAX's collectives and lax.ppermute only.
A program may use at most 192 MiB of HBM per device.

```python
import math
import jax
import jax.numpy as jnp
import numpy as np
from jax import lax

D = 1536
HEADS = 16
KV_HEADS = 8
HEAD_DIM = 96
FF = 4096
MICRO = 2
SEQS = 4
LAYERS = 2
MB_TOK = 1024
LONGEST = 896


def spiked(entries, rng, source, target, parts, factor):
    owner, partner = [(jnp.arange(entries.shape[axis_at]) // (entries.shape[axis_at] // parts)).reshape([-1 if axis == axis_at else 1 for axis in range(entries.ndim)]) for axis_at in (source, target)]
    chosen = jax.random.permutation(rng, parts)[partner]
    strong = (owner == chosen) | (owner == (partner + parts // 2) % parts)
    return jnp.where(strong, factor * entries, entries)


def levels(key, shape, split, low, high):
    level = 1.0
    for dim, shards_of in split:
        draws = jax.random.uniform(jax.random.fold_in(jax.random.fold_in(key, 6), dim), (shards_of,), jnp.float32, low / len(split), high / len(split))
        level = level * jnp.repeat(jnp.exp(draws), shape[dim] // shards_of).reshape((-1,) + (1,) * (len(shape) - 1 - dim))
    return level


def split_up(amount, total, limit, lean):
    loads = [(1 << 20) // math.isqrt(grade ** lean) + 1 for grade in range(2, amount + 1)]
    rest, holding = total - limit - (amount - 1), [1] * (amount - 1)
    while rest > 0:
        free = [i for i in range(amount - 1) if holding[i] < limit]
        whole, left = sum([loads[i] for i in free]), rest
        for i in free:
            more = min(limit - holding[i], max(1, left * loads[i] // whole), rest)
            holding[i] = holding[i] + more
            rest = rest - more
    return np.array([limit] + holding)


def uneven(key, amount, total, limit, skew):
    if amount == 2:
        one = jax.random.randint(key, (), max(1, total - limit), min(limit, total - 1) + 1)
        return jnp.stack([one, total - one])
    sizes = jnp.asarray(split_up(amount, total, limit, skew), jnp.int32)
    couples = (amount - 1) // 2
    giver, sink = sizes[1:1 + 2 * couples:2], sizes[2:2 + 2 * couples:2]
    slack = jnp.minimum(giver - 1, limit - sink)
    shifted = jax.random.randint(jax.random.fold_in(key, 1), (couples,), 0, 1 << 20) % (slack + 1)
    sizes = sizes.at[1:1 + 2 * couples:2].set(giver - shifted).at[2:2 + 2 * couples:2].set(sink + shifted)
    return sizes[jax.random.permutation(jax.random.fold_in(key, 2), amount)]


def gaussian(rng, extent, deviation, limit, split=(), kind=jnp.bfloat16):
    factor_of = levels(rng, extent, split, -0.22, 0.18) if split else 1.0
    drawn = jax.random.normal(rng, extent, jnp.float32) * deviation * factor_of
    return jnp.minimum(jnp.maximum(drawn, -limit), limit).astype(kind)


def heavy_noise(key, shape, scale, bound, pieces, heavy, kind=jnp.bfloat16):
    entries = scale * jax.random.normal(key, shape, jnp.float32)
    if pieces:
        entries = entries * levels(key, shape, pieces, -0.22, 0.18)
    return jnp.clip(spiked(entries, jax.random.fold_in(key, 3), *heavy), -bound, bound).astype(kind)


def setup_inputs(seed: int = 0) -> dict:
    key_list = jax.random.split(jax.random.key(seed), 13)
    layer_input = heavy_noise(key_list[0], (MICRO, MB_TOK, D), 1.0, 6.0, ((1, 4),), (1, 2, 4, 2.0))
    seq_lengths = jax.vmap(lambda own: uneven(own, SEQS, MB_TOK, LONGEST, 2))(jax.random.split(key_list[1], MICRO)).reshape((MICRO, SEQS)).astype(jnp.int32)
    norm1_gain = jnp.clip(1.0 + 0.18 * jax.random.normal(key_list[2], (LAYERS, D), jnp.float32), 0.1, 1.9)
    w_query = gaussian(key_list[3], (LAYERS, D, HEADS * HEAD_DIM), D ** -0.5, 0.15625, ((0, 2), (2, 4)))
    w_key = gaussian(key_list[4], (LAYERS, D, KV_HEADS * HEAD_DIM), D ** -0.5, 0.15625, ((0, 2), (2, 4)))
    w_value = gaussian(key_list[5], (LAYERS, D, KV_HEADS * HEAD_DIM), D ** -0.5, 0.15625, ((0, 2), (2, 4)))
    w_out = gaussian(key_list[6], (LAYERS, HEADS * HEAD_DIM, D), 32 ** -0.5, 1.0, ((0, 2), (1, 4)))
    norm2_gain = jnp.clip(1.0 + 0.18 * jax.random.normal(key_list[7], (LAYERS, D), jnp.float32), 0.1, 1.9)
    w_gate = gaussian(key_list[8], (LAYERS, D, FF), D ** -0.5, 0.15625, ((0, 2), (2, 4)))
    w_up = gaussian(key_list[9], (LAYERS, D, FF), D ** -0.5, 0.15625, ((0, 2), (2, 4)))
    w_down = gaussian(key_list[10], (LAYERS, FF, D), FF ** -0.5, 0.09375, ((0, 2), (1, 4)))
    out_grad = heavy_noise(key_list[11], (MICRO, MB_TOK, D), 1.0, 6.0, ((1, 4),), (1, 2, 4, 2.0))
    return {"layer_input": layer_input, "seq_lengths": seq_lengths, "norm1_gain": norm1_gain, "w_query": w_query, "w_key": w_key, "w_value": w_value, "w_out": w_out, "norm2_gain": norm2_gain, "w_gate": w_gate, "w_up": w_up, "w_down": w_down, "out_grad": out_grad}


EPS = 1e-05
THETA = 100000.0
MASKED = -1e+30

@jax.custom_vjp
def low(v):
    return lax.optimization_barrier(v.astype(jnp.bfloat16)).astype(jnp.float32)

@jax.custom_vjp
def low_back(v):
    return v

def low_keep(v):
    return (low(v), None)

def low_pass(kept, grad):
    return (grad,)

def back_keep(v):
    return (v, None)

def back_low(kept, grad):
    return (low(grad),)
low.defvjp(low_keep, low_pass)
low_back.defvjp(back_keep, back_low)

def matmul(left, right):
    return jnp.dot(left, right, precision=lax.Precision.HIGHEST, preferred_element_type=jnp.float32)

def layout(lengths):
    seq_ends = jnp.cumsum(lengths).astype(jnp.int32)
    starts = seq_ends - lengths
    places = jnp.arange(MB_TOK, dtype=jnp.int32)
    segment = lax.optimization_barrier(jnp.sum((places[:, None] >= seq_ends[None, :]).astype(jnp.int32), axis=1))
    labels = jnp.arange(SEQS, dtype=jnp.int32)
    offset = lax.optimization_barrier(jnp.sum(jnp.where(segment[:, None] == labels[None, :], starts[None, :], 0), axis=1))
    return (segment, places - offset)

def rotate(per_head, position, direction):
    head_size = per_head.shape[-1]
    halfway = head_size // 2
    inverse = THETA ** (-2.0 * jnp.arange(halfway, dtype=jnp.float32) / head_size)
    angles = position.astype(jnp.float32)[:, None] * inverse[None, :]
    cosine = jnp.cos(angles)[:, None, :]
    sine_part = direction * jnp.sin(angles)[:, None, :]
    leading = per_head[..., :halfway]
    trailing = per_head[..., halfway:]
    return jnp.concatenate([leading * cosine - trailing * sine_part, trailing * cosine + leading * sine_part], axis=-1)

def rms_norm(values, gain):
    return values * lax.rsqrt(lax.optimization_barrier(jnp.mean(values * values, axis=-1, keepdims=True)) + EPS) * gain

def attend(queries, key_rows, value_rows, segment):
    group_size = HEADS // KV_HEADS
    key_all = jnp.repeat(key_rows, group_size, axis=1)
    value_all = jnp.repeat(value_rows, group_size, axis=1)
    block_rows = min(512, MB_TOK)
    places = jnp.arange(MB_TOK, dtype=jnp.int32)
    factor = HEAD_DIM ** (-0.5)

    def one_block(block_index):
        first_row = block_index * block_rows
        query_block = lax.dynamic_slice_in_dim(queries, first_row, block_rows, 0)
        seg_rows = lax.dynamic_slice_in_dim(segment, first_row, block_rows, 0)
        place_rows = first_row + jnp.arange(block_rows, dtype=jnp.int32)
        raw = jnp.einsum('qhd,khd->hqk', query_block, key_all, precision=lax.Precision.HIGHEST)
        scores = low_back(raw) * factor
        allowed = (seg_rows[:, None] == segment[None, :]) & (places[None, :] <= place_rows[:, None])
        scores = jnp.where(allowed[None], scores, MASKED)
        chances = jax.nn.softmax(scores, axis=-1)
        return jnp.einsum('hqk,khd->qhd', low(chances), value_all, precision=lax.Precision.HIGHEST)
    blocks = lax.map(jax.checkpoint(one_block), jnp.arange(MB_TOK // block_rows, dtype=jnp.int32))
    return blocks.reshape(MB_TOK, HEADS, HEAD_DIM)

def layer(hidden_in, segment, position, params):
    gain_one, query_weight, key_weight, value_weight, out_weight, gain_two, gate_weight, up_weight, down_weight = params
    normed_one = low(rms_norm(hidden_in, gain_one))
    queries = low(rotate(low_back(matmul(normed_one, query_weight)).reshape(MB_TOK, HEADS, HEAD_DIM), position, 1.0))
    key_rows = low(rotate(low_back(matmul(normed_one, key_weight)).reshape(MB_TOK, KV_HEADS, HEAD_DIM), position, 1.0))
    value_rows = low(low_back(matmul(normed_one, value_weight))).reshape(MB_TOK, KV_HEADS, HEAD_DIM)
    mixed = low(low_back(attend(queries, key_rows, value_rows, segment))).reshape(MB_TOK, HEADS * HEAD_DIM)
    middle = hidden_in + low_back(matmul(mixed, out_weight))
    normed_two = low(rms_norm(middle, gain_two))
    gate = low_back(matmul(normed_two, gate_weight))
    upward = low_back(matmul(normed_two, up_weight))
    hidden_act = low(jax.nn.silu(gate) * upward)
    return middle + low_back(matmul(hidden_act, down_weight))

def reference(layer_input, seq_lengths, norm1_gain, w_query, w_key, w_value, w_out, norm2_gain, w_gate, w_up, w_down, out_grad):
    weights = tuple((array_in.astype(jnp.float32) for array_in in (norm1_gain, w_query, w_key, w_value, w_out, norm2_gain, w_gate, w_up, w_down)))
    inputs = layer_input.astype(jnp.float32)
    bridges = jnp.zeros((LAYERS - 1, MICRO, MB_TOK, D), jnp.float32)

    def forward(inputs, bridges, weights):
        per_micro = []
        for micro_index in range(MICRO):
            segment, position = layout(seq_lengths[micro_index])
            current = inputs[micro_index]
            sent_list = []
            for layer_index in range(LAYERS):
                if layer_index > 0:
                    current = low_back(current + bridges[layer_index - 1, micro_index])
                params = tuple((array_in[layer_index] for array_in in weights))
                sent = low(layer(current, segment, position, params))
                sent_list.append(sent)
                current = sent
            per_micro.append(jnp.stack(sent_list))
        return jnp.stack(per_micro, axis=1)
    outputs, pullback = jax.vjp(forward, inputs, bridges, weights)
    cotangent = jnp.concatenate([jnp.zeros((LAYERS - 1, MICRO, MB_TOK, D), jnp.float32), out_grad.astype(jnp.float32)[None]], axis=0)
    input_grad, bridge_grad, weight_grads = pullback(cotangent)
    input_grads = jnp.concatenate([input_grad[None], bridge_grad], axis=0).astype(jnp.bfloat16)
    return (outputs.astype(jnp.bfloat16), input_grads, weight_grads[0], weight_grads[1], weight_grads[2], weight_grads[3], weight_grads[4], weight_grads[5], weight_grads[6], weight_grads[7], weight_grads[8])
```

```python
import functools

import jax
import jax.numpy as jnp
from jax import lax
from jax.experimental import pallas as pl
from jax.experimental.pallas import tpu as pltpu
from jax.sharding import PartitionSpec as P

HEAD_DIM = 96
EPS = 1e-05
THETA = 100000.0
MASKED = -1e30
BF = jnp.bfloat16
F32 = jnp.float32
FACTOR = HEAD_DIM ** (-0.5)
CHUNKS = 2
TILE = 256
AHEAD = 6


def dot(left, right):
    return jnp.dot(left, right, preferred_element_type=F32)


def dot_t(left, right):
    return lax.dot_general(left, right, (((1,), (1,)), ((), ())), preferred_element_type=F32)


def outer(left, right):
    return lax.dot_general(left, right, (((0,), (0,)), ((), ())), preferred_element_type=F32)


def swap(value):
    return lax.ppermute(value, "section", [(0, 1), (1, 0)])


def shape(dims, dtype):
    return jax.ShapeDtypeStruct(dims, dtype)


VMEM = pl.BlockSpec(memory_space=pltpu.VMEM)
ANY = pl.BlockSpec(memory_space=pl.ANY)
NEAR, FAR, RAW, LOOSE, LOOSE_RAW = "near", "far", "raw", "loose", "loose raw"


class Late:
    def __init__(self, source, buffer, sem):
        self.buffer = buffer
        self.copy = pltpu.make_async_copy(source, buffer, sem)
        self.copy.start()
        self.waited = False

    def __getitem__(self, index):
        if not self.waited:
            self.copy.wait()
            self.waited = True
        return self.buffer[index]


class Leaving:
    def __init__(self, buffer, target, sem):
        self.buffer, self.target, self.sem = buffer, target, sem
        self.copy = pltpu.make_async_copy(buffer, target, sem)
        self.started = False

    def __setitem__(self, index, value):
        self.buffer[index] = value

    def __getitem__(self, index):
        return self.buffer[index]

    def send(self, *parts):
        if parts:
            for index in parts:
                pltpu.make_async_copy(self.buffer.at[index], self.target.at[index], self.sem).start()
        elif not self.started:
            self.copy.start()
        self.started = True


def fixed(value, where):
    if where in (LOOSE, LOOSE_RAW):
        return value
    return pltpu.with_memory_space_constraint(value, pltpu.VMEM if where == NEAR else pltpu.HBM)


class Order:
    token = ()


def kernel_call(body, name, ins, outs, scratch=(), after=(), cost=1.0, limit=24):
    after = [*after, *Order.token]
    far_in = [i for i, (_, where) in enumerate(ins) if where in (FAR, LOOSE)]
    far_out = [i for i, (_, where) in enumerate(outs) if where == FAR]
    buffers = [pltpu.VMEM(ins[i][0].shape, ins[i][0].dtype) for i in far_in]
    buffers += [pltpu.VMEM(outs[i][0].shape, outs[i][0].dtype) for i in far_out]
    count = len(far_in) + len(far_out)
    if count:
        buffers.append(pltpu.SemaphoreType.DMA((count,)))

    def whole(*refs):
        refs = list(refs)
        in_refs, refs = refs[: len(ins)], refs[len(ins) + len(after) :]
        out_refs, refs = refs[: len(outs)], refs[len(outs) :]
        own, refs = refs[: len(buffers)], refs[len(buffers) :]
        for place, index in enumerate(far_in):
            in_refs[index] = Late(in_refs[index], own[place], own[-1].at[place])
        for place, index in enumerate(far_out, len(far_in)):
            out_refs[index] = Leaving(own[place], out_refs[index], own[-1].at[place])
        body(in_refs, out_refs, *refs)
        for index in far_in:
            in_refs[index][0:1]
        for index in far_out:
            out_refs[index].send()
        for index in far_out:
            out_refs[index].copy.wait()

    call = pl.pallas_call(
        whole,
        out_shape=[
            pltpu.VMEM(out.shape, out.dtype) if where == NEAR else pltpu.HBM(out.shape, out.dtype)
            for out, where in outs
        ],
        in_specs=[VMEM if where == NEAR else ANY for _, where in ins] + [ANY] * len(after),
        out_specs=[VMEM if where == NEAR else ANY for _, where in outs],
        scratch_shapes=buffers + list(scratch),
        compiler_params=pltpu.CompilerParams(vmem_limit_bytes=limit * 1024 * 1024),
        cost_estimate=pl.CostEstimate(flops=int(cost * 1e9), bytes_accessed=0, transcendentals=0),
        name=name,
    )
    results = call(*[fixed(value, where) for value, where in [*ins, *after]])
    best = min(range(len(outs)), key=lambda index: outs[index][0].size)
    Order.token = ((results[best], NEAR if outs[best][1] == NEAR else RAW),)
    return results


def near(values):
    return [(value, NEAR) for value in values]


def far(values):
    return [(value, FAR) for value in values]


def raw(values):
    return [(value, RAW) for value in values]


def loose(values):
    return [(value, LOOSE) for value in values]


def weights(pairs):
    return raw([weight for pair in pairs for weight in pair])


def fetch(layer, copies):
    mine = lax.axis_index("section") == layer

    @pl.when(mine)
    def _():
        for own, _, buffer, sem in copies:
            pltpu.make_async_copy(own, buffer, sem).start()

    @pl.when(jnp.logical_not(mine))
    def _():
        for _, other, buffer, sem in copies:
            pltpu.make_async_copy(other, buffer, sem).start()


def arrived(own, buffer, sem):
    pltpu.make_async_copy(own, buffer, sem).wait()


def is_middle():
    index = lax.axis_index("tensor")
    return (index == 1) | (index == 2)


def summed(refs):
    middle = is_middle()
    parts = []
    for index in range(CHUNKS):
        parts.append(jnp.where(middle, refs[2 * index][...], refs[2 * index + 1][...]))
    return jnp.concatenate(parts, axis=1).astype(F32)


def store_chunks(value, refs):
    size = value.shape[1] // len(refs)
    for index, ref in enumerate(refs):
        ref[...] = value[:, index * size : (index + 1) * size].astype(BF)


def store_halves(value, mine_out, theirs_out):
    half = value.shape[1] // 2
    early = lax.axis_index("section") == 0
    left, right = value[:, :half], value[:, half:]
    mine_out[...] = jnp.where(early, left, right)
    theirs_out[...] = jnp.where(early, right, left)


def norm_scale(values):
    return lax.rsqrt(jnp.mean(values * values, axis=-1, keepdims=True) + EPS)


def norm_back(values, scale, gain, grad):
    weighted = grad * gain
    coupling = jnp.mean(weighted * values, axis=-1, keepdims=True)
    return scale * weighted - values * (scale * scale * scale * coupling)


def rotate(flat, cosine, sine):
    width = flat.shape[1]
    half = HEAD_DIM // 2
    lane = lax.broadcasted_iota(jnp.int32, flat.shape, 1) % HEAD_DIM
    partner = jnp.where(
        lane < half, pltpu.roll(flat, width - half, 1), pltpu.roll(flat, half, 1)
    )
    return flat * cosine + partner * sine


def key_tables(cosine, sine):
    lane = lax.broadcasted_iota(jnp.int32, cosine.shape, 1)
    is_key = lane < cosine.shape[1] // 2
    return jnp.where(is_key, cosine, 1.0), jnp.where(is_key, sine, 0.0)


def qkv_copies(wq, wk, wv, q_buf, kv_buf, sem):
    kv = wk[0].shape[1]
    return [
        (wq[0].at[0], wq[1].at[0], q_buf, sem.at[0]),
        (wk[0].at[0], wk[1].at[0], kv_buf.at[pl.ds(0, kv)], sem.at[1]),
        (wv[0].at[0], wv[1].at[0], kv_buf.at[pl.ds(kv, kv)], sem.at[2]),
    ]


def norm_qkv(layer, first, ins, outs, q_buf, kv_buf, sem):
    gain, cosine, sine = ins[:3]
    wq, wk, wv = ins[3:5], ins[5:7], ins[7:9]
    query_out, kv_out, normed_out = outs[:3]
    copies = qkv_copies(wq, wk, wv, q_buf, kv_buf, sem)
    fetch(layer, copies)
    if first:
        hidden = ins[9][...].astype(F32)
    else:
        low = (ins[9][...] + summed(ins[10:])).astype(BF)
        outs[3][...] = low
        outs[3].send()
        hidden = low.astype(F32)
    normed = (hidden * norm_scale(hidden) * gain[...]).astype(BF)
    normed_out[...] = normed
    normed_out.send()
    cos, sin = cosine[...], sine[...]
    key_cos, key_sin = key_tables(cos, sin)
    for own, _, buffer, one in copies:
        arrived(own, buffer, one)
    kv_out[...] = rotate(dot_t(normed, kv_buf[...]), key_cos, key_sin).astype(BF)
    kv_out.send()
    query_out[...] = rotate(dot(normed, q_buf[...]), cos, sin).astype(BF)


def split_keys(kv_refs, k_buf, v_buf):
    groups = k_buf.shape[0]
    rows = k_buf.shape[1] // len(kv_refs)
    for index, ref in enumerate(kv_refs):
        block = ref[...]
        for group in range(groups):
            low = group * HEAD_DIM
            k_buf[group, index * rows : (index + 1) * rows, :] = block[:, low : low + HEAD_DIM]
            low = (groups + group) * HEAD_DIM
            v_buf[group, index * rows : (index + 1) * rows, :] = block[:, low : low + HEAD_DIM]


def attention(layer, peers, ins, outs, q_buf, k_buf, v_buf, wo_buf, sem):
    wo, wo_other, query, bias = ins[:4]
    kv_refs = ins[4:]
    mine_out, theirs_out, attn_out, lse_out = outs[:4]
    fetch(layer, [(wo.at[0], wo_other.at[0], wo_buf, sem)])
    heads = q_buf.shape[0]
    group_size = heads // k_buf.shape[0]
    split_query(query[...], q_buf)
    split_keys(kv_refs, k_buf, v_buf)
    results, totals = [], []
    for head in range(heads):
        group = head // group_size
        scores = dot_t(q_buf[head], k_buf[group]) * FACTOR + bias[...]
        top = jnp.max(scores, axis=-1, keepdims=True)
        weights = jnp.exp(scores - top)
        total = jnp.sum(weights, axis=-1, keepdims=True)
        totals.append(top + jnp.log(total))
        chances = (weights * (1.0 / total)).astype(BF)
        results.append(dot(chances, v_buf[group]))
    attn = jnp.concatenate(results, axis=1)
    attn_out[...] = attn
    attn_out.send()
    lse_out[...] = jnp.concatenate(totals, axis=1)
    rows = attn.astype(BF)
    store_halves(rows, mine_out, theirs_out)
    arrived(wo.at[0], wo_buf, sem)
    store_chunks(dot(rows, wo_buf[...]), outs[4:])


def split_query(query, q_buf):
    for head in range(q_buf.shape[0]):
        q_buf[head] = query[:, head * HEAD_DIM : (head + 1) * HEAD_DIM]


def mlp_copies(wg, wu, wd, g_buf, u_buf, d_buf, sem):
    copies = []
    for step in range(g_buf.shape[0]):
        part = pl.ds(step * TILE, TILE)
        copies.append((wg[0].at[0, :, part], wg[1].at[0, :, part], g_buf.at[step], sem.at[0, step]))
        copies.append((wu[0].at[0, :, part], wu[1].at[0, :, part], u_buf.at[step], sem.at[1, step]))
        copies.append((wd[0].at[0, part, :], wd[1].at[0, part, :], d_buf.at[step], sem.at[2, step]))
    return copies


def mlp(layer, ins, outs, g_buf, u_buf, d_buf, total, act_buf, sem):
    wg, wu, wd = ins[0:2], ins[2:4], ins[4:6]
    hidden, gain = ins[6:8]
    middle_out, normed_out, gate_out, up_out, mine_out, theirs_out = outs[:6]
    copies = mlp_copies(wg, wu, wd, g_buf, u_buf, d_buf, sem)
    fetch(layer, copies[:AHEAD])
    middle = hidden[...].astype(F32) + summed(ins[8:])
    middle_out[...] = middle
    middle_out.send()
    normed_out[...] = (middle * norm_scale(middle) * gain[...]).astype(BF)
    normed_out.send()
    for step in range(g_buf.shape[0]):
        if len(copies) > 3 * step + AHEAD:
            fetch(layer, copies[3 * step + AHEAD : 3 * step + 3 + AHEAD])
        for own, _, buffer, one in copies[3 * step : 3 * step + 3]:
            arrived(own, buffer, one)
        part = slice(step * TILE, (step + 1) * TILE)
        gate = dot(normed_out[...], g_buf[step])
        upward = dot(normed_out[...], u_buf[step])
        gate_out[:, part] = gate
        up_out[:, part] = upward
        act = (gate * jax.nn.sigmoid(gate) * upward).astype(BF)
        gate_out.send((slice(None), part))
        up_out.send((slice(None), part))
        act_buf[:, part] = act
        term = dot(act, d_buf[step])
        if step == 0:
            total[...] = term
        else:
            total[...] += term
    store_halves(act_buf[...], mine_out, theirs_out)
    theirs_out.send()
    mine_out.send()
    store_chunks(total[...], outs[6:])


def mlp_back(layer, last, ins, outs, g_buf, u_buf, d_buf, total, sem):
    wg, wu, wd = ins[0:2], ins[2:4], ins[4:6]
    gate_ref, up_ref = ins[6:8]
    mine_out, theirs_out = outs[:2]
    chunks = outs[2 : 2 + CHUNKS]
    copies = mlp_copies(wg, wu, wd, g_buf, u_buf, d_buf, sem)
    fetch(layer, copies[:AHEAD])
    early = lax.axis_index("section") == 0
    if last:
        grad_ref = ins[8]
    else:
        middle_grad, hidden, gain = ins[8:11]
        grad_ref, gain_out = outs[2 + CHUNKS :]
        values, grad = hidden[...].astype(F32), summed(ins[11:])
        scale = norm_scale(values)
        gain_out[...] = jnp.sum(grad * values * scale, axis=0, keepdims=True)
        grad_ref[...] = (middle_grad[...] + norm_back(values, scale, gain[...], grad)).astype(BF)
        grad_ref.send()
    for step in range(g_buf.shape[0]):
        if len(copies) > 3 * step + AHEAD:
            fetch(layer, copies[3 * step + AHEAD : 3 * step + 3 + AHEAD])
        for own, _, buffer, one in copies[3 * step : 3 * step + 3]:
            arrived(own, buffer, one)
        part = slice(step * TILE, (step + 1) * TILE)
        act_grad = dot_t(grad_ref[...], d_buf[step])
        gate, upward = gate_ref[:, part], up_ref[:, part]
        sigma = jax.nn.sigmoid(gate)
        gate_grad = (act_grad * upward * sigma * (1.0 + gate * (1.0 - sigma))).astype(BF)
        up_grad = (act_grad * gate * sigma).astype(BF)
        mine_out[:, part] = jnp.where(early, gate_grad, up_grad)
        theirs_out[:, part] = jnp.where(early, up_grad, gate_grad)
        theirs_out.send((slice(None), part))
        mine_out.send((slice(None), part))
        term = dot_t(gate_grad, g_buf[step]) + dot_t(up_grad, u_buf[step])
        if step == 0:
            total[...] = term
        else:
            total[...] += term
    store_chunks(total[...], chunks)


def attention_back(layer, peers, ins, outs, q_buf, k_buf, v_buf, dk_buf, dv_buf, wo_buf, sem):
    wo, wo_other, grad_in, middle, gain, query, bias, attn, lse, cosine, sine = ins[:11]
    kv_refs, sums = ins[11 : 11 + peers], ins[11 + peers :]
    middle_grad_out, low_out, gain_out, pre_out = outs[:4]
    block_outs = outs[4:]
    fetch(layer, [(wo.at[0], wo_other.at[0], wo_buf, sem)])
    heads, groups = q_buf.shape[0], k_buf.shape[0]
    group_size = heads // groups
    grad = summed(sums)
    values = middle[...]
    scale = norm_scale(values)
    gain_out[...] = jnp.sum(grad * values * scale, axis=0, keepdims=True)
    middle_grad = grad_in[...].astype(F32) + norm_back(values, scale, gain[...], grad)
    middle_grad_out[...] = middle_grad
    middle_grad_out.send()
    low_out[...] = middle_grad.astype(BF)
    low_out.send()
    arrived(wo.at[0], wo_buf, sem)
    attn_grad = dot_t(low_out[...], wo_buf[...]).astype(BF)
    split_query(query[...], q_buf)
    split_keys(kv_refs, k_buf, v_buf)
    query_grads = []
    for head in range(heads):
        group = head // group_size
        lanes = slice(head * HEAD_DIM, (head + 1) * HEAD_DIM)
        head_grad = attn_grad[:, lanes]
        delta = jnp.sum(head_grad.astype(F32) * attn[:, lanes], axis=-1, keepdims=True)
        scores = dot_t(q_buf[head], k_buf[group]) * FACTOR + bias[...]
        chances = jnp.exp(scores - lse[:, head : head + 1])
        chance_grad = dot_t(head_grad, v_buf[group])
        score_grad = (chances * (chance_grad - delta) * FACTOR).astype(BF)
        query_grads.append(dot(score_grad, k_buf[group]))
        key_term = outer(score_grad, q_buf[head])
        value_term = outer(chances.astype(BF), head_grad)
        if head % group_size == 0:
            dk_buf[group] = key_term
            dv_buf[group] = value_term
        else:
            dk_buf[group] += key_term
            dv_buf[group] += value_term
    rows = middle_grad.shape[0]
    for index in reversed(range(peers)):
        span = slice(index * rows, (index + 1) * rows)
        block = jnp.concatenate(
            [dk_buf[group, span, :] for group in range(groups)]
            + [dv_buf[group, span, :] for group in range(groups)],
            axis=1,
        )
        block_outs[index][...] = block if index == 0 else block.astype(BF)
        block_outs[index].send()
    query_grad = jnp.concatenate(query_grads, axis=1)
    pre_out[...] = rotate(query_grad, cosine[...], -sine[...]).astype(BF)


def qkv_back(layer, ins, outs, q_buf, kv_buf, sem):
    wq, wk, wv = ins[0:2], ins[2:4], ins[4:6]
    pre_query, cosine, sine, own = ins[6:10]
    mine_out, theirs_out = outs[:2]
    copies = qkv_copies(wq, wk, wv, q_buf, kv_buf, sem)
    fetch(layer, copies)
    both = own[...]
    for ref in ins[10:]:
        both = both + ref[...].astype(F32)
    key_cos, key_sin = key_tables(cosine[...], sine[...])
    pre = rotate(both, key_cos, -key_sin).astype(BF)
    early = lax.axis_index("section") == 0
    pre_q = pre_query[...]
    mine_out[...] = jnp.where(early, pre_q, pre)
    theirs_out[...] = jnp.where(early, pre, pre_q)
    theirs_out.send()
    mine_out.send()
    for own_weight, _, buffer, one in copies:
        arrived(own_weight, buffer, one)
    store_chunks(dot_t(pre_q, q_buf[...]) + dot(pre, kv_buf[...]), outs[2:])


def finish(ins, outs):
    middle_grad, hidden, gain = ins[:3]
    values, grad = hidden[...].astype(F32), summed(ins[3:])
    scale = norm_scale(values)
    outs[0][...] = (middle_grad[...] + norm_back(values, scale, gain[...], grad)).astype(BF)
    outs[0].send()
    outs[1][...] = jnp.sum(grad * values * scale, axis=0, keepdims=True)


def grad_blocks(spread, ins, outs, *scratch):
    buffer = scratch[0] if spread else outs[0]
    peers = len(outs) if spread else outs[0].buffer.shape[0]
    me = lax.axis_index("dp")
    start = 0
    for left, left_other, right, right_other in zip(*[iter(ins)] * 4):
        wide, wide_other = right[...], right_other[...]
        size = left.buffer.shape[1] // peers
        lanes = slice(start, start + wide.shape[1])
        for block in range(peers):
            span = slice(block * size, (block + 1) * size)
            term = outer(left[:, span], wide) + outer(left_other[:, span], wide_other)
            place = lax.bitwise_xor(me, block) if spread else block
            buffer[place, :, lanes] = term.astype(BF)
        start += wide.shape[1]
    if spread:
        for index, out in enumerate(outs):
            out[...] = buffer[index]
            out.send()


def add_blocks(ins, outs):
    total = ins[0][...].astype(F32)
    for block in ins[1:]:
        total = total + block[...].astype(F32)
    outs[0][...] = total.astype(BF)


def grad_parts(kept, received):
    early = lax.axis_index("section") == 0

    def halves(lanes):
        own, other = kept[:, lanes].astype(F32), received[:, lanes].astype(F32)
        return jnp.where(early, own, other), jnp.where(early, other, own)

    return halves


def mlp_grads(ins, outs):
    halves = grad_parts(*ins)
    gate_out, up_out, down_out = outs
    ff = gate_out.buffer.shape[1]
    gate, upward = halves(slice(0, ff))
    gate_out[...] = gate
    gate_out.send()
    up_out[...] = upward
    up_out.send()
    half = ff // 2
    for index, part in enumerate(halves(slice(ff, ff + half))):
        down_out[index * half : (index + 1) * half, :] = part.T


def head_grads(ins, outs):
    halves = grad_parts(*ins)
    out_out, query_out, key_out, value_out = outs
    half = out_out.buffer.shape[0] // 2
    for index, part in enumerate(halves(slice(0, half))):
        out_out[index * half : (index + 1) * half, :] = part.T
    query, key_value = halves(slice(half, 3 * half))
    query_out[...] = query
    flipped = key_value.T
    key_out[...] = flipped[:half]
    value_out[...] = flipped[half:]


def copy_body(ins, outs):
    outs[0][...] = ins[0][...]


def held(value, after):
    (out,) = kernel_call(
        copy_body, "held", far([value]), near([shape(value.shape, value.dtype)]), after=after
    )
    return out


def add_rounded(ins, outs):
    outs[0][...] = (ins[0][...].astype(F32) + ins[1][...].astype(F32)).astype(BF)


def add(left, right, after=()):
    (out,) = kernel_call(
        add_rounded, "add", near([left, right]), near([shape(left.shape, BF)]), after=after, cost=0.2
    )
    return out


def hop_in(parts):
    return [lax.ppermute(part, "tensor", [(0, 1), (3, 2)]) for part in parts]


def hop_across(parts):
    return [lax.ppermute(part, "tensor", [(1, 2), (2, 1)]) for part in parts]


def hop_out(parts):
    return [lax.ppermute(part, "tensor", [(1, 0), (2, 3)]) for part in parts]


def add_all(parts, others, after=()):
    return [add(part, other, after) for part, other in zip(parts, others)]


def sum_tensor(parts):
    pairs = add_all(parts, hop_in(parts))
    totals = add_all(pairs, hop_across(pairs))
    return [piece for both in zip(totals, hop_out(totals)) for piece in both]


def layout(lengths, token_count):
    seq_ends = jnp.cumsum(lengths)
    starts = seq_ends - lengths
    places = jnp.arange(token_count, dtype=jnp.int32)
    segment = jnp.sum((places[:, None] >= seq_ends[None, :]).astype(jnp.int32), axis=1)
    labels = jnp.arange(lengths.shape[0], dtype=jnp.int32)
    offset = jnp.sum(jnp.where(segment[:, None] == labels[None, :], starts[None, :], 0), axis=1)
    return (segment, places - offset)


def rope_tables(position, heads):
    halfway = HEAD_DIM // 2
    inverse = THETA ** (-2.0 * jnp.arange(halfway, dtype=F32) / HEAD_DIM)
    angles = position.astype(F32)[:, None] * inverse[None, :]
    cosine, sine = jnp.cos(angles), jnp.sin(angles)
    return (
        jnp.tile(jnp.concatenate([cosine, cosine], axis=-1), (1, heads)),
        jnp.tile(jnp.concatenate([-sine, sine], axis=-1), (1, heads)),
    )


def peer_pairs(peers, step, later):
    pairs = [(low, low ^ step) for low in range(peers) if low < low ^ step]
    return [(high, low) for low, high in pairs] if later else pairs


def per_device(
    layer_input,
    seq_lengths,
    norm1_gain,
    w_query,
    w_key,
    w_value,
    w_out,
    norm2_gain,
    w_gate,
    w_up,
    w_down,
    out_grad,
):
    Order.token = ()
    rows, width = layer_input.shape[1:]
    peers = lax.axis_size("dp")
    me = lax.axis_index("dp")
    first = lax.axis_index("section") == 0
    q_width, kv_width, ff = w_query.shape[2], w_key.shape[2], w_gate.shape[2]
    heads, groups = q_width // HEAD_DIM, kv_width // HEAD_DIM
    tokens = rows * peers
    steps = ff // TILE
    part = width // CHUNKS

    def pick(early, late):
        return jnp.where(first, early, late)

    own = [w_query, jnp.swapaxes(w_key, 1, 2), jnp.swapaxes(w_value, 1, 2), w_out, w_gate, w_up, w_down]
    pairs = [(weight, swap(weight)) for weight in own]
    wq, wk, wv, wo, wg, wu, wd = pairs
    gains = []
    for gain in (norm1_gain, norm2_gain):
        other = swap(gain)
        gains.append((pick(gain, other), pick(other, gain)))

    segment, position = layout(pick(seq_lengths[0], seq_lengths[1]), tokens)
    row_seg = lax.dynamic_slice_in_dim(segment, me * rows, rows, 0)
    row_pos = lax.dynamic_slice_in_dim(position, me * rows, rows, 0)
    local = jnp.arange(rows, dtype=jnp.int32)
    key_place = jnp.concatenate([(me ^ step) * rows + local for step in range(peers)])
    key_seg = jnp.concatenate(
        [lax.dynamic_slice_in_dim(segment, (me ^ step) * rows, rows, 0) for step in range(peers)]
    )
    allowed = (row_seg[:, None] == key_seg[None, :]) & (
        key_place[None, :] <= (me * rows + local)[:, None]
    )
    bias = jnp.where(allowed, 0.0, MASKED).astype(F32)
    cosine, sine = rope_tables(row_pos, heads)

    chunk_outs = near([shape((rows, part), BF)] * CHUNKS)
    row_f32 = shape((rows, width), F32)
    row_bf = shape((rows, width), BF)
    line = shape((1, width), F32)
    head_bf = shape((rows, q_width), BF)
    half_head = shape((rows, q_width // 2), BF)
    half_wide = shape((rows, ff // 2), BF)
    kv_bf = shape((rows, 2 * kv_width), BF)
    wide_f32 = shape((rows, ff), F32)
    wide_bf = shape((rows, ff), BF)
    dma = pltpu.SemaphoreType.DMA
    qkv_scratch = [
        pltpu.VMEM((width, q_width), BF),
        pltpu.VMEM((2 * kv_width, width), BF),
        dma((3,)),
    ]
    mlp_scratch = [
        pltpu.VMEM((steps, width, TILE), BF),
        pltpu.VMEM((steps, width, TILE), BF),
        pltpu.VMEM((steps, TILE, width), BF),
        pltpu.VMEM((rows, width), F32),
        dma((3, steps)),
    ]
    head_scratch = [
        pltpu.VMEM((heads, rows, HEAD_DIM), BF),
        pltpu.VMEM((groups, tokens, HEAD_DIM), BF),
        pltpu.VMEM((groups, tokens, HEAD_DIM), BF),
    ]

    def run_qkv(layer, source, sums):
        start = layer == 0
        outs = [head_bf, kv_bf, row_bf]
        return kernel_call(
            functools.partial(norm_qkv, layer, start),
            f"norm_qkv_{layer}",
            far([gains[0][layer], cosine, sine]) + weights([wq, wk, wv]) + far([source]) + near(sums),
            far(outs if start else outs + [row_bf]),
            qkv_scratch,
            cost=4.0,
        )

    def run_attention(layer, query, blocks):
        outs = [half_head] * 2 + [shape((rows, q_width), F32), shape((rows, heads), F32)]
        return kernel_call(
            functools.partial(attention, layer, peers),
            f"attention_{layer}",
            weights([wo]) + far([query, bias, *blocks]),
            far(outs) + chunk_outs,
            head_scratch + [pltpu.VMEM((q_width, width), BF), dma],
            cost=5.0,
            limit=min(8 + 4 * peers, 56),
        )

    def run_mlp(layer, hidden, sums):
        return kernel_call(
            functools.partial(mlp, layer),
            f"mlp_{layer}",
            weights([wg, wu, wd]) + far([hidden, gains[1][layer]]) + near(sums),
            far([row_f32, row_bf, wide_f32, wide_f32, half_wide, half_wide])
            + (chunk_outs if layer == 0 else far([row_bf])),
            mlp_scratch[:-1] + [pltpu.VMEM((rows, ff), BF)] + mlp_scratch[-1:],
            cost=6.0,
            limit=32,
        )

    def run_mlp_back(layer, source, sums, gate, upward, after):
        last = layer == 1
        outs = far([wide_bf, wide_bf]) + chunk_outs
        return kernel_call(
            functools.partial(mlp_back, layer, last),
            f"mlp_back_{layer}",
            weights([wg, wu, wd]) + far([gate, upward, *source]) + near(sums),
            outs if last else outs + far([row_bf, line]),
            mlp_scratch,
            after,
            cost=8.0,
            limit=32,
        )

    def run_attention_back(layer, grad, middle, sums, query, blocks, attn, lse, after):
        return kernel_call(
            functools.partial(attention_back, layer, peers),
            f"attention_back_{layer}",
            weights([wo])
            + far([grad, middle, gains[1][layer], query, bias, attn, lse, cosine, sine, *blocks])
            + near(sums),
            far([row_f32, row_bf, line, head_bf, shape((rows, 2 * kv_width), F32)] + [kv_bf] * (peers - 1)),
            head_scratch
            + [
                pltpu.VMEM((groups, tokens, HEAD_DIM), F32),
                pltpu.VMEM((groups, tokens, HEAD_DIM), F32),
                pltpu.VMEM((q_width, width), BF),
                dma,
            ],
            after,
            cost=9.0,
            limit=min(16 + 4 * peers, 56),
        )

    def run_qkv_back(layer, pre_query, pieces, after):
        return kernel_call(
            functools.partial(qkv_back, layer),
            f"qkv_back_{layer}",
            weights([wq, wk, wv]) + far([pre_query, cosine, sine]) + loose(pieces),
            far([kv_bf, kv_bf]) + chunk_outs,
            qkv_scratch,
            after,
            cost=4.0,
        )

    def weight_grad(groups, name, spread):
        ins, tall = [], 0
        for left, left_other, mine, mine_other in groups:
            ins += far([left]) + loose([left_other]) + far([mine]) + loose([mine_other])
            tall += mine.shape[1]
        block = shape((width // peers, tall), BF)
        whole = shape((peers, width // peers, tall), BF)
        blocks = kernel_call(
            functools.partial(grad_blocks, spread),
            name,
            ins,
            far([block] * peers if spread else [whole]),
            [pltpu.VMEM(whole.shape, BF)] if spread else [],
            cost=8.0,
        )
        if not spread:
            return blocks, lax.psum_scatter(blocks[0], "dp", scatter_dimension=0, tiled=False)
        pieces = [blocks[0]]
        for step in range(1, peers):
            pairing = [(peer, peer ^ step) for peer in range(peers)]
            pieces.append(lax.ppermute(blocks[step], "dp", pairing))

        def total():
            return kernel_call(
                add_blocks, "add_" + name, far(pieces[:1]) + loose(pieces[1:]), far([block])
            )[0]

        return blocks, total

    def whole_grads(body, name, per_layer, dims):
        kept = pick(per_layer[0], per_layer[1])
        received = swap(pick(per_layer[1], per_layer[0]))
        return kernel_call(
            body, name, loose([kept, received]), far([shape(dim, F32) for dim in dims]), cost=4.0
        )

    def by_layer(per_layer):
        received = swap(pick(per_layer[1], per_layer[0]))
        kept = pick(per_layer[0], per_layer[1])
        return jnp.stack([pick(kept, received), pick(received, kept)])[None]

    hidden = pick(layer_input[0], layer_input[1])
    grad = pick(out_grad[0], out_grad[1])
    saved, outputs = [], []
    for layer in range(2):
        if layer == 0:
            query, kv, normed_one = run_qkv(layer, hidden, [])
        else:
            query, kv, normed_one, hidden = run_qkv(layer, middle, sums)
            outputs.append(hidden)
        blocks = [kv]
        for step in range(1, peers):
            blocks.append(lax.ppermute(kv, "dp", peer_pairs(peers, step, False)))
        *head_halves, attn, lse, chunk_one, chunk_two = run_attention(layer, query, blocks)
        sums = sum_tensor([chunk_one, chunk_two])
        middle, normed_two, gate, upward, act_mine, act_theirs, *parts = run_mlp(
            layer, hidden, sums
        )
        act_halves = [act_mine, act_theirs]
        if layer == 0:
            sums = sum_tensor(parts)
        saved.append(
            (hidden, query, blocks, normed_one, head_halves, attn, lse)
            + (middle, normed_two, gate, upward, act_halves)
        )

    last_middle, last_part = middle, parts[0]
    in_grads, vectors, mlp_parts, head_parts = [None, None], [None, None], [None, None], [None, None]
    source, sums = [grad], []
    for layer in (1, 0):
        (hidden, query, blocks, normed_one, head_halves, attn, lse) = saved[layer][:7]
        (middle, normed_two, gate, upward, act_halves) = saved[layer][7:]
        if layer == 1:
            mine, theirs, *parts = run_mlp_back(layer, source, sums, gate, upward, [])
        else:
            mine, theirs, *parts, grad, gain_one = run_mlp_back(
                layer, source, sums, gate, upward, []
            )
            in_grads[1] = grad
        inward = hop_in(parts)
        mlp_blocks, mlp_parts[layer] = weight_grad(
            [
                (normed_two, swap(normed_two), mine, swap(theirs)),
                (grad, swap(grad), act_halves[0], swap(act_halves[1])),
            ],
            f"grad_mlp_{layer}",
            False,
        )
        pairs = add_all(parts, inward)
        totals = add_all(pairs, hop_across(pairs))
        outward = hop_out(totals)
        sums = [piece for both in zip(totals, outward) for piece in both]
        if layer == 1:
            last_part = held(last_part, [])
            (last_inward,) = hop_in([last_part])
        else:
            last_total = add(last_pair, last_across)
            (last_outward,) = hop_out([last_total])
        middle_grad, low, gain_two, pre_query, *pieces = run_attention_back(
            layer, grad, middle, sums, query, blocks, attn, lse, []
        )
        far_pieces = [
            lax.ppermute(pieces[step], "dp", peer_pairs(peers, step, True))
            for step in range(1, peers)
        ]
        if layer == 1:
            last_pair = add(last_part, last_inward)
            (last_across,) = hop_across([last_pair])
        mine, theirs, *parts = run_qkv_back(layer, pre_query, [pieces[0]] + far_pieces, [])
        inward = hop_in(parts)
        head_blocks, head_parts[layer] = weight_grad(
            [
                (low, swap(low), head_halves[0], swap(head_halves[1])),
                (normed_one, swap(normed_one), mine, swap(theirs)),
            ],
            f"grad_head_{layer}",
            layer == 0,
        )
        pairs = add_all(parts, inward)
        totals = add_all(pairs, hop_across(pairs))
        outward = hop_out(totals)
        sums = [piece for both in zip(totals, outward) for piece in both]
        source = [middle_grad, hidden, gains[0][layer]]
        vectors[layer] = gain_two
    in_grads[0], last_line = kernel_call(
        finish, "finish", far(source) + near(sums), far([row_bf, line])
    )
    lines = jnp.concatenate([last_line, vectors[0], gain_one, vectors[1]], axis=0)
    for axis in ("section", "dp"):
        for bit in range((lax.axis_size(axis) - 1).bit_length()):
            pairing = [(peer, peer ^ (1 << bit)) for peer in range(lax.axis_size(axis))]
            lines = lines + lax.ppermute(lines, axis, pairing)

    at_middle = (lax.axis_index("tensor") == 1) | (lax.axis_index("tensor") == 2)
    last_sum = jnp.where(at_middle, last_total, last_outward)
    outputs.append((last_middle + last_sum.astype(F32)).astype(BF))
    activations = by_layer(outputs)
    input_grads = by_layer(in_grads)
    size = width // peers
    head_parts[0] = head_parts[0]()
    grad_gate, grad_up, grad_down = whole_grads(
        mlp_grads, "mlp_grads", mlp_parts, [(size, ff), (size, ff), (ff, size)]
    )
    grad_out, grad_query, grad_key, grad_value = whole_grads(
        head_grads,
        "head_grads",
        head_parts,
        [(q_width, size), (size, q_width), (kv_width, size), (kv_width, size)],
    )
    grad_key, grad_value = grad_key.T, grad_value.T
    lines = lax.dynamic_slice_in_dim(lines, me * size, size, 1)
    return (
        activations,
        input_grads,
        pick(lines[0], lines[2])[None],
        grad_query[None],
        grad_key[None],
        grad_value[None],
        grad_out[None],
        pick(lines[1], lines[3])[None],
        grad_gate[None],
        grad_up[None],
        grad_down[None],
    )


def solution(mesh):
    placed = (
        P(None, "dp", None),
        P(),
        P("section", None),
        P("section", None, "tensor"),
        P("section", None, "tensor"),
        P("section", None, "tensor"),
        P("section", "tensor", None),
        P("section", None),
        P("section", None, "tensor"),
        P("section", None, "tensor"),
        P("section", "tensor", None),
        P(None, "dp", None),
    )
    return jax.shard_map(
        per_device,
        mesh=mesh,
        in_specs=placed,
        out_specs=(
            P("section", None, "dp", None),
            P("section", None, "dp", None),
            P("section", "dp"),
            P("section", "dp", "tensor"),
            P("section", "dp", "tensor"),
            P("section", "dp", "tensor"),
            P("section", "tensor", "dp"),
            P("section", "dp"),
            P("section", "dp", "tensor"),
            P("section", "dp", "tensor"),
            P("section", "tensor", "dp"),
        ),
        check_vma=False,
    )
```

```python
import functools

import jax
import jax.numpy as jnp
from jax import lax
from jax.experimental import pallas as pl
from jax.experimental.pallas import tpu as pltpu
from jax.sharding import PartitionSpec as P

HEAD_DIM = 96
EPS = 1e-05
THETA = 100000.0
MASKED = -1e30
BF = jnp.bfloat16
F32 = jnp.float32
FACTOR = HEAD_DIM ** (-0.5)
TILE = 256
AHEAD = 6


def dot(left, right):
    return jnp.dot(left, right, preferred_element_type=F32)


def dot_t(left, right):
    return lax.dot_general(left, right, (((1,), (1,)), ((), ())), preferred_element_type=F32)


def outer(left, right):
    return lax.dot_general(left, right, (((0,), (0,)), ((), ())), preferred_element_type=F32)


def swap(value):
    return lax.ppermute(value, "section", [(0, 1), (1, 0)])


def shape(dims, dtype):
    return jax.ShapeDtypeStruct(dims, dtype)


VMEM = pl.BlockSpec(memory_space=pltpu.VMEM)
ANY = pl.BlockSpec(memory_space=pl.ANY)
NEAR, FAR, RAW, LOOSE, LOOSE_RAW = "near", "far", "raw", "loose", "loose raw"


class Late:
    def __init__(self, source, buffer, sem):
        self.buffer = buffer
        self.copy = pltpu.make_async_copy(source, buffer, sem)
        self.copy.start()
        self.waited = False

    def __getitem__(self, index):
        if not self.waited:
            self.copy.wait()
            self.waited = True
        return self.buffer[index]


class Leaving:
    def __init__(self, buffer, target, sem):
        self.buffer, self.target, self.sem = buffer, target, sem
        self.copy = pltpu.make_async_copy(buffer, target, sem)
        self.started = False

    def __setitem__(self, index, value):
        self.buffer[index] = value

    def __getitem__(self, index):
        return self.buffer[index]

    def send(self, *parts):
        if parts:
            for index in parts:
                pltpu.make_async_copy(self.buffer.at[index], self.target.at[index], self.sem).start()
        elif not self.started:
            self.copy.start()
        self.started = True


def fixed(value, where):
    if where in (LOOSE, LOOSE_RAW):
        return value
    return pltpu.with_memory_space_constraint(value, pltpu.VMEM if where == NEAR else pltpu.HBM)


class Order:
    token = ()
    pending = []


def soon(value):
    other = swap(value)
    Order.pending.append(other)
    return other


def collect():
    values, Order.pending = Order.pending, []
    return [(value, LOOSE_RAW) for value in values]


def kernel_call(body, name, ins, outs, scratch=(), after=(), cost=1.0, limit=24):
    after = [*after, *Order.token]
    far_in = [i for i, (_, where) in enumerate(ins) if where in (FAR, LOOSE)]
    far_out = [i for i, (_, where) in enumerate(outs) if where == FAR]
    buffers = [pltpu.VMEM(ins[i][0].shape, ins[i][0].dtype) for i in far_in]
    buffers += [pltpu.VMEM(outs[i][0].shape, outs[i][0].dtype) for i in far_out]
    count = len(far_in) + len(far_out)
    if count:
        buffers.append(pltpu.SemaphoreType.DMA((count,)))

    def whole(*refs):
        refs = list(refs)
        in_refs, refs = refs[: len(ins)], refs[len(ins) + len(after) :]
        out_refs, refs = refs[: len(outs)], refs[len(outs) :]
        own, refs = refs[: len(buffers)], refs[len(buffers) :]
        for place, index in enumerate(far_in):
            in_refs[index] = Late(in_refs[index], own[place], own[-1].at[place])
        for place, index in enumerate(far_out, len(far_in)):
            out_refs[index] = Leaving(own[place], out_refs[index], own[-1].at[place])
        body(in_refs, out_refs, *refs)
        for index in far_in:
            in_refs[index][0:1]
        for index in far_out:
            out_refs[index].send()
        for index in far_out:
            out_refs[index].copy.wait()

    call = pl.pallas_call(
        whole,
        out_shape=[
            pltpu.VMEM(out.shape, out.dtype) if where == NEAR else pltpu.HBM(out.shape, out.dtype)
            for out, where in outs
        ],
        in_specs=[VMEM if where == NEAR else ANY for _, where in ins] + [ANY] * len(after),
        out_specs=[VMEM if where == NEAR else ANY for _, where in outs],
        scratch_shapes=buffers + list(scratch),
        compiler_params=pltpu.CompilerParams(vmem_limit_bytes=limit * 1024 * 1024),
        cost_estimate=pl.CostEstimate(flops=int(cost * 1e9), bytes_accessed=0, transcendentals=0),
        name=name,
    )
    results = call(*[fixed(value, where) for value, where in [*ins, *after]])
    best = min(range(len(outs)), key=lambda index: outs[index][0].size)
    Order.token = ((results[best], NEAR if outs[best][1] == NEAR else RAW),)
    return results


def near(values):
    return [(value, NEAR) for value in values]


def far(values):
    return [(value, FAR) for value in values]


def raw(values):
    return [(value, RAW) for value in values]


def loose(values):
    return [(value, LOOSE) for value in values]


def weights(pairs):
    return raw([weight for pair in pairs for weight in pair])


def fetch(layer, copies):
    mine = lax.axis_index("section") == layer

    @pl.when(mine)
    def _():
        for own, _, buffer, sem in copies:
            pltpu.make_async_copy(own, buffer, sem).start()

    @pl.when(jnp.logical_not(mine))
    def _():
        for _, other, buffer, sem in copies:
            pltpu.make_async_copy(other, buffer, sem).start()


def arrived(own, buffer, sem):
    pltpu.make_async_copy(own, buffer, sem).wait()


def share_of(step, size):
    start = lax.bitwise_xor(lax.axis_index("tensor"), step) * size
    return pl.ds(pl.multiple_of(start, size), size)


def summed(refs, buffer):
    for step, ref in enumerate(refs):
        buffer[share_of(step, ref.shape[0]), :] = ref[...]
    return buffer[...].astype(F32)


def store_shares(total, refs):
    size = total.shape[0] // len(refs)
    for step, ref in enumerate(refs):
        ref[...] = total[share_of(step, size), :].astype(BF)


def store_halves(value, mine_out, theirs_out):
    half = value.shape[1] // 2
    early = lax.axis_index("section") == 0
    left, right = value[:, :half], value[:, half:]
    mine_out[...] = jnp.where(early, left, right)
    theirs_out[...] = jnp.where(early, right, left)


def norm_scale(values):
    return lax.rsqrt(jnp.mean(values * values, axis=-1, keepdims=True) + EPS)


def norm_back(values, scale, gain, grad):
    weighted = grad * gain
    coupling = jnp.mean(weighted * values, axis=-1, keepdims=True)
    return scale * weighted - values * (scale * scale * scale * coupling)


def rotate(flat, cosine, sine):
    width = flat.shape[1]
    half = HEAD_DIM // 2
    lane = lax.broadcasted_iota(jnp.int32, flat.shape, 1) % HEAD_DIM
    partner = jnp.where(
        lane < half, pltpu.roll(flat, width - half, 1), pltpu.roll(flat, half, 1)
    )
    return flat * cosine + partner * sine


def key_tables(cosine, sine):
    lane = lax.broadcasted_iota(jnp.int32, cosine.shape, 1)
    is_key = lane < cosine.shape[1] // 2
    return jnp.where(is_key, cosine, 1.0), jnp.where(is_key, sine, 0.0)


def qkv_copies(wq, wk, wv, q_buf, kv_buf, sem):
    kv = wk[0].shape[1]
    return [
        (wq[0].at[0], wq[1].at[0], q_buf, sem.at[0]),
        (wk[0].at[0], wk[1].at[0], kv_buf.at[pl.ds(0, kv)], sem.at[1]),
        (wv[0].at[0], wv[1].at[0], kv_buf.at[pl.ds(kv, kv)], sem.at[2]),
    ]


def norm_qkv(layer, first, ins, outs, q_buf, kv_buf, rows_buf, sem):
    gain, cosine, sine = ins[:3]
    wq, wk, wv = ins[3:5], ins[5:7], ins[7:9]
    query_out, kv_out, normed_out = outs[:3]
    copies = qkv_copies(wq, wk, wv, q_buf, kv_buf, sem)
    fetch(layer, copies)
    if first:
        hidden = ins[9][...].astype(F32)
    else:
        low = (ins[9][...] + summed(ins[10:], rows_buf)).astype(BF)
        outs[3][...] = low
        outs[3].send()
        hidden = low.astype(F32)
    normed = (hidden * norm_scale(hidden) * gain[...]).astype(BF)
    normed_out[...] = normed
    normed_out.send()
    cos, sin = cosine[...], sine[...]
    key_cos, key_sin = key_tables(cos, sin)
    for own, _, buffer, one in copies:
        arrived(own, buffer, one)
    kv_out[...] = rotate(dot_t(normed, kv_buf[...]), key_cos, key_sin).astype(BF)
    kv_out.send()
    query_out[...] = rotate(dot(normed, q_buf[...]), cos, sin).astype(BF)


def split_keys(kv_refs, k_buf, v_buf):
    groups = k_buf.shape[0]
    rows = k_buf.shape[1] // len(kv_refs)
    for index, ref in enumerate(kv_refs):
        block = ref[...]
        for group in range(groups):
            low = group * HEAD_DIM
            k_buf[group, index * rows : (index + 1) * rows, :] = block[:, low : low + HEAD_DIM]
            low = (groups + group) * HEAD_DIM
            v_buf[group, index * rows : (index + 1) * rows, :] = block[:, low : low + HEAD_DIM]


def attention(layer, peers, ins, outs, q_buf, k_buf, v_buf, wo_buf, sum_buf, sem):
    wo, wo_other, query, bias = ins[:4]
    kv_refs = ins[4:]
    mine_out, theirs_out, attn_out, lse_out = outs[:4]
    fetch(layer, [(wo.at[0], wo_other.at[0], wo_buf, sem)])
    heads = q_buf.shape[0]
    group_size = heads // k_buf.shape[0]
    split_query(query[...], q_buf)
    split_keys(kv_refs, k_buf, v_buf)
    results, totals = [], []
    for head in range(heads):
        group = head // group_size
        scores = dot_t(q_buf[head], k_buf[group]) * FACTOR + bias[...]
        top = jnp.max(scores, axis=-1, keepdims=True)
        weights = jnp.exp(scores - top)
        total = jnp.sum(weights, axis=-1, keepdims=True)
        totals.append(top + jnp.log(total))
        chances = (weights * (1.0 / total)).astype(BF)
        results.append(dot(chances, v_buf[group]))
    attn = jnp.concatenate(results, axis=1)
    attn_out[...] = attn
    attn_out.send()
    lse_out[...] = jnp.concatenate(totals, axis=1)
    rows = attn.astype(BF)
    store_halves(rows, mine_out, theirs_out)
    arrived(wo.at[0], wo_buf, sem)
    sum_buf[...] = dot(rows, wo_buf[...])
    store_shares(sum_buf, outs[4:])


def split_query(query, q_buf):
    for head in range(q_buf.shape[0]):
        q_buf[head] = query[:, head * HEAD_DIM : (head + 1) * HEAD_DIM]


def mlp_copies(wg, wu, wd, g_buf, u_buf, d_buf, sem):
    copies = []
    for step in range(g_buf.shape[0]):
        part = pl.ds(step * TILE, TILE)
        copies.append((wg[0].at[0, :, part], wg[1].at[0, :, part], g_buf.at[step], sem.at[0, step]))
        copies.append((wu[0].at[0, :, part], wu[1].at[0, :, part], u_buf.at[step], sem.at[1, step]))
        copies.append((wd[0].at[0, part, :], wd[1].at[0, part, :], d_buf.at[step], sem.at[2, step]))
    return copies


def mlp(layer, ins, outs, g_buf, u_buf, d_buf, total, rows_buf, act_buf, sem):
    wg, wu, wd = ins[0:2], ins[2:4], ins[4:6]
    hidden, gain = ins[6:8]
    middle_out, normed_out, gate_out, up_out, mine_out, theirs_out = outs[:6]
    copies = mlp_copies(wg, wu, wd, g_buf, u_buf, d_buf, sem)
    fetch(layer, copies[:AHEAD])
    middle = hidden[...].astype(F32) + summed(ins[8:], rows_buf)
    middle_out[...] = middle
    middle_out.send()
    normed_out[...] = (middle * norm_scale(middle) * gain[...]).astype(BF)
    normed_out.send()
    for step in range(g_buf.shape[0]):
        if len(copies) > 3 * step + AHEAD:
            fetch(layer, copies[3 * step + AHEAD : 3 * step + 3 + AHEAD])
        for own, _, buffer, one in copies[3 * step : 3 * step + 3]:
            arrived(own, buffer, one)
        part = slice(step * TILE, (step + 1) * TILE)
        gate = dot(normed_out[...], g_buf[step])
        upward = dot(normed_out[...], u_buf[step])
        gate_out[:, part] = gate
        up_out[:, part] = upward
        act = (gate * jax.nn.sigmoid(gate) * upward).astype(BF)
        gate_out.send((slice(None), part))
        up_out.send((slice(None), part))
        act_buf[:, part] = act
        term = dot(act, d_buf[step])
        if step == 0:
            total[...] = term
        else:
            total[...] += term
    store_halves(act_buf[...], mine_out, theirs_out)
    theirs_out.send()
    mine_out.send()
    store_shares(total, outs[6:])


def mlp_back(layer, last, ins, outs, g_buf, u_buf, d_buf, total, rows_buf, sem):
    wg, wu, wd = ins[0:2], ins[2:4], ins[4:6]
    gate_ref, up_ref = ins[6:8]
    mine_out, theirs_out = outs[:2]
    shares = outs[2:] if last else outs[2:-2]
    copies = mlp_copies(wg, wu, wd, g_buf, u_buf, d_buf, sem)
    fetch(layer, copies[:AHEAD])
    early = lax.axis_index("section") == 0
    if last:
        grad_ref = ins[8]
    else:
        middle_grad, hidden, gain = ins[8:11]
        grad_ref, gain_out = outs[-2:]
        values, grad = hidden[...].astype(F32), summed(ins[11:], rows_buf)
        scale = norm_scale(values)
        gain_out[...] = jnp.sum(grad * values * scale, axis=0, keepdims=True)
        grad_ref[...] = (middle_grad[...] + norm_back(values, scale, gain[...], grad)).astype(BF)
        grad_ref.send()
    for step in range(g_buf.shape[0]):
        if len(copies) > 3 * step + AHEAD:
            fetch(layer, copies[3 * step + AHEAD : 3 * step + 3 + AHEAD])
        for own, _, buffer, one in copies[3 * step : 3 * step + 3]:
            arrived(own, buffer, one)
        part = slice(step * TILE, (step + 1) * TILE)
        act_grad = dot_t(grad_ref[...], d_buf[step])
        gate, upward = gate_ref[:, part], up_ref[:, part]
        sigma = jax.nn.sigmoid(gate)
        gate_grad = (act_grad * upward * sigma * (1.0 + gate * (1.0 - sigma))).astype(BF)
        up_grad = (act_grad * gate * sigma).astype(BF)
        mine_out[:, part] = jnp.where(early, gate_grad, up_grad)
        theirs_out[:, part] = jnp.where(early, up_grad, gate_grad)
        theirs_out.send((slice(None), part))
        mine_out.send((slice(None), part))
        term = dot_t(gate_grad, g_buf[step]) + dot_t(up_grad, u_buf[step])
        if step == 0:
            total[...] = term
        else:
            total[...] += term
    store_shares(total, shares)


def attention_back(layer, peers, ins, outs, q_buf, k_buf, v_buf, dk_buf, dv_buf, wo_buf, rows_buf, sem):
    wo, wo_other, grad_in, middle, gain, query, bias, attn, lse, cosine, sine = ins[:11]
    kv_refs, sums = ins[11 : 11 + peers], ins[11 + peers :]
    middle_grad_out, low_out, gain_out, pre_out = outs[:4]
    block_outs = outs[4:]
    fetch(layer, [(wo.at[0], wo_other.at[0], wo_buf, sem)])
    heads, groups = q_buf.shape[0], k_buf.shape[0]
    group_size = heads // groups
    grad = summed(sums, rows_buf)
    values = middle[...]
    scale = norm_scale(values)
    gain_out[...] = jnp.sum(grad * values * scale, axis=0, keepdims=True)
    middle_grad = grad_in[...].astype(F32) + norm_back(values, scale, gain[...], grad)
    middle_grad_out[...] = middle_grad
    middle_grad_out.send()
    low_out[...] = middle_grad.astype(BF)
    low_out.send()
    arrived(wo.at[0], wo_buf, sem)
    attn_grad = dot_t(low_out[...], wo_buf[...]).astype(BF)
    split_query(query[...], q_buf)
    split_keys(kv_refs, k_buf, v_buf)
    query_grads = []
    for head in range(heads):
        group = head // group_size
        lanes = slice(head * HEAD_DIM, (head + 1) * HEAD_DIM)
        head_grad = attn_grad[:, lanes]
        delta = jnp.sum(head_grad.astype(F32) * attn[:, lanes], axis=-1, keepdims=True)
        scores = dot_t(q_buf[head], k_buf[group]) * FACTOR + bias[...]
        chances = jnp.exp(scores - lse[:, head : head + 1])
        chance_grad = dot_t(head_grad, v_buf[group])
        score_grad = (chances * (chance_grad - delta) * FACTOR).astype(BF)
        query_grads.append(dot(score_grad, k_buf[group]))
        key_term = outer(score_grad, q_buf[head])
        value_term = outer(chances.astype(BF), head_grad)
        if head % group_size == 0:
            dk_buf[group] = key_term
            dv_buf[group] = value_term
        else:
            dk_buf[group] += key_term
            dv_buf[group] += value_term
    rows = middle_grad.shape[0]
    for index in reversed(range(peers)):
        span = slice(index * rows, (index + 1) * rows)
        block = jnp.concatenate(
            [dk_buf[group, span, :] for group in range(groups)]
            + [dv_buf[group, span, :] for group in range(groups)],
            axis=1,
        )
        block_outs[index][...] = block if index == 0 else block.astype(BF)
        block_outs[index].send()
    query_grad = jnp.concatenate(query_grads, axis=1)
    pre_out[...] = rotate(query_grad, cosine[...], -sine[...]).astype(BF)


def qkv_back(layer, ins, outs, q_buf, kv_buf, total, sem):
    wq, wk, wv = ins[0:2], ins[2:4], ins[4:6]
    pre_query, cosine, sine, own = ins[6:10]
    mine_out, theirs_out = outs[:2]
    copies = qkv_copies(wq, wk, wv, q_buf, kv_buf, sem)
    fetch(layer, copies)
    both = own[...]
    for ref in ins[10:]:
        both = both + ref[...].astype(F32)
    key_cos, key_sin = key_tables(cosine[...], sine[...])
    pre = rotate(both, key_cos, -key_sin).astype(BF)
    early = lax.axis_index("section") == 0
    pre_q = pre_query[...]
    mine_out[...] = jnp.where(early, pre_q, pre)
    theirs_out[...] = jnp.where(early, pre, pre_q)
    theirs_out.send()
    mine_out.send()
    for own_weight, _, buffer, one in copies:
        arrived(own_weight, buffer, one)
    total[...] = dot_t(pre_q, q_buf[...]) + dot(pre, kv_buf[...])
    store_shares(total, outs[2:])


def last_output(ins, outs, rows_buf):
    outs[0][...] = (ins[0][...] + summed(ins[1:], rows_buf)).astype(BF)


def finish(ins, outs, rows_buf):
    middle_grad, hidden, gain = ins[:3]
    values, grad = hidden[...].astype(F32), summed(ins[3:], rows_buf)
    scale = norm_scale(values)
    outs[0][...] = (middle_grad[...] + norm_back(values, scale, gain[...], grad)).astype(BF)
    outs[0].send()
    outs[1][...] = jnp.sum(grad * values * scale, axis=0, keepdims=True)


def grad_blocks(spread, ins, outs, *scratch):
    buffer = scratch[0] if spread else outs[0].buffer
    peers = len(outs) if spread else outs[0].buffer.shape[0]
    me = lax.axis_index("dp")
    start = 0
    for left, left_other, right, right_other in zip(*[iter(ins)] * 4):
        wide, wide_other = right[...], right_other[...]
        size = left.buffer.shape[1] // peers
        lanes = slice(start, start + wide.shape[1])
        for block in range(peers):
            span = slice(block * size, (block + 1) * size)
            term = outer(left[:, span], wide) + outer(left_other[:, span], wide_other)
            place = lax.bitwise_xor(me, block) if spread else block
            buffer[place, :, lanes] = term.astype(BF)
        start += wide.shape[1]
    if start < buffer.shape[-1]:
        rest = buffer.shape[-1] - start
        buffer[:, :, start:] = jnp.zeros((peers, buffer.shape[1], rest), BF)
    if spread:
        for index, out in enumerate(outs):
            out[...] = buffer[index]
            out.send()


def add_blocks(ins, outs):
    total = ins[0][...].astype(F32)
    for block in ins[1:]:
        total = total + block[...].astype(F32)
    outs[0][...] = total.astype(BF)


def grad_parts(kept, received):
    early = lax.axis_index("section") == 0

    def halves(lanes):
        own, other = kept[:, lanes].astype(F32), received[:, lanes].astype(F32)
        return jnp.where(early, own, other), jnp.where(early, other, own)

    return halves


def mlp_grads(ins, outs):
    halves = grad_parts(*ins)
    gate_out, up_out, down_out = outs
    ff = gate_out.buffer.shape[1]
    gate, upward = halves(slice(0, ff))
    gate_out[...] = gate
    gate_out.send()
    up_out[...] = upward
    up_out.send()
    half = ff // 2
    for index, part in enumerate(halves(slice(ff, ff + half))):
        down_out[index * half : (index + 1) * half, :] = part.T


def head_grads(ins, outs):
    halves = grad_parts(*ins)
    out_out, query_out, key_out, value_out = outs
    half = out_out.buffer.shape[0] // 2
    for index, part in enumerate(halves(slice(0, half))):
        out_out[index * half : (index + 1) * half, :] = part.T
    query, key_value = halves(slice(half, 3 * half))
    query_out[...] = query
    flipped = key_value.T
    key_out[...] = flipped[:half]
    value_out[...] = flipped[half:]


def add_shares(ins, outs):
    total = ins[0][...].astype(F32)
    for ref in ins[1:]:
        total = total + ref[...].astype(F32)
    outs[0][...] = total.astype(BF)


def spread(values):
    peers = len(values)
    return [values[0]] + [
        lax.ppermute(values[step], "tensor", [(peer, peer ^ step) for peer in range(peers)])
        for step in range(1, peers)
    ]


def add_rows(received, after=()):
    (total,) = kernel_call(
        add_shares,
        "add_shares",
        near(received),
        near([shape(received[0].shape, BF)]),
        after=after,
        cost=0.5,
    )
    return total


def sum_tensor(parts):
    return spread([add_rows(spread(parts))] * len(parts))


def layout(lengths, token_count):
    seq_ends = jnp.cumsum(lengths)
    starts = seq_ends - lengths
    places = jnp.arange(token_count, dtype=jnp.int32)
    segment = jnp.sum((places[:, None] >= seq_ends[None, :]).astype(jnp.int32), axis=1)
    labels = jnp.arange(lengths.shape[0], dtype=jnp.int32)
    offset = jnp.sum(jnp.where(segment[:, None] == labels[None, :], starts[None, :], 0), axis=1)
    return (segment, places - offset)


def rope_tables(position, heads):
    halfway = HEAD_DIM // 2
    inverse = THETA ** (-2.0 * jnp.arange(halfway, dtype=F32) / HEAD_DIM)
    angles = position.astype(F32)[:, None] * inverse[None, :]
    cosine, sine = jnp.cos(angles), jnp.sin(angles)
    return (
        jnp.tile(jnp.concatenate([cosine, cosine], axis=-1), (1, heads)),
        jnp.tile(jnp.concatenate([-sine, sine], axis=-1), (1, heads)),
    )


def peer_pairs(peers, step, later):
    pairs = [(low, low ^ step) for low in range(peers) if low < low ^ step]
    return [(high, low) for low, high in pairs] if later else pairs


def per_device(
    layer_input,
    seq_lengths,
    norm1_gain,
    w_query,
    w_key,
    w_value,
    w_out,
    norm2_gain,
    w_gate,
    w_up,
    w_down,
    out_grad,
):
    Order.token, Order.pending = (), []
    rows, width = layer_input.shape[1:]
    peers = lax.axis_size("dp")
    me = lax.axis_index("dp")
    first = lax.axis_index("section") == 0
    q_width, kv_width, ff = w_query.shape[2], w_key.shape[2], w_gate.shape[2]
    heads, groups = q_width // HEAD_DIM, kv_width // HEAD_DIM
    tokens = rows * peers
    steps = ff // TILE
    shares = lax.axis_size("tensor")

    def pick(early, late):
        return jnp.where(first, early, late)

    own = [w_query, jnp.swapaxes(w_key, 1, 2), jnp.swapaxes(w_value, 1, 2), w_out, w_gate, w_up, w_down]
    pairs = [(weight, swap(weight)) for weight in own]
    wq, wk, wv, wo, wg, wu, wd = pairs
    gains = []
    for gain in (norm1_gain, norm2_gain):
        other = swap(gain)
        gains.append((pick(gain, other), pick(other, gain)))

    segment, position = layout(pick(seq_lengths[0], seq_lengths[1]), tokens)
    row_seg = lax.dynamic_slice_in_dim(segment, me * rows, rows, 0)
    row_pos = lax.dynamic_slice_in_dim(position, me * rows, rows, 0)
    local = jnp.arange(rows, dtype=jnp.int32)
    key_place = jnp.concatenate([(me ^ step) * rows + local for step in range(peers)])
    key_seg = jnp.concatenate(
        [lax.dynamic_slice_in_dim(segment, (me ^ step) * rows, rows, 0) for step in range(peers)]
    )
    allowed = (row_seg[:, None] == key_seg[None, :]) & (
        key_place[None, :] <= (me * rows + local)[:, None]
    )
    bias = jnp.where(allowed, 0.0, MASKED).astype(F32)
    cosine, sine = rope_tables(row_pos, heads)

    share = shape((rows // shares, width), BF)
    share_outs = near([share] * shares)
    rows_buf = pltpu.VMEM((rows, width), BF)
    total_buf = pltpu.VMEM((rows, width), F32)
    row_f32 = shape((rows, width), F32)
    row_bf = shape((rows, width), BF)
    line = shape((1, width), F32)
    head_bf = shape((rows, q_width), BF)
    half_head = shape((rows, q_width // 2), BF)
    half_wide = shape((rows, ff // 2), BF)
    kv_bf = shape((rows, 2 * kv_width), BF)
    wide_f32 = shape((rows, ff), F32)
    wide_bf = shape((rows, ff), BF)
    dma = pltpu.SemaphoreType.DMA
    qkv_scratch = [
        pltpu.VMEM((width, q_width), BF),
        pltpu.VMEM((2 * kv_width, width), BF),
    ]
    mlp_scratch = [
        pltpu.VMEM((steps, width, TILE), BF),
        pltpu.VMEM((steps, width, TILE), BF),
        pltpu.VMEM((steps, TILE, width), BF),
        total_buf,
        rows_buf,
    ]
    head_scratch = [
        pltpu.VMEM((heads, rows, HEAD_DIM), BF),
        pltpu.VMEM((groups, tokens, HEAD_DIM), BF),
        pltpu.VMEM((groups, tokens, HEAD_DIM), BF),
    ]

    def run_qkv(layer, source, sums, after):
        start = layer == 0
        outs = [head_bf, kv_bf, row_bf]
        return kernel_call(
            functools.partial(norm_qkv, layer, start),
            f"norm_qkv_{layer}",
            far([gains[0][layer], cosine, sine]) + weights([wq, wk, wv]) + far([source]) + near(sums),
            far(outs if start else outs + [row_bf]),
            qkv_scratch + [rows_buf, dma((3,))],
            after,
            cost=4.0,
        )

    def run_attention(layer, query, blocks, after):
        outs = [half_head] * 2 + [shape((rows, q_width), F32), shape((rows, heads), F32)]
        return kernel_call(
            functools.partial(attention, layer, peers),
            f"attention_{layer}",
            weights([wo]) + far([query, bias, *blocks]),
            far(outs) + share_outs,
            head_scratch + [pltpu.VMEM((q_width, width), BF), total_buf, dma],
            after,
            cost=5.0,
            limit=min(8 + 4 * peers, 56),
        )

    def run_mlp(layer, hidden, sums, after):
        return kernel_call(
            functools.partial(mlp, layer),
            f"mlp_{layer}",
            weights([wg, wu, wd]) + far([hidden, gains[1][layer]]) + near(sums),
            far([row_f32, row_bf, wide_f32, wide_f32, half_wide, half_wide])
            + (share_outs if layer == 0 else far([share] * shares)),
            mlp_scratch + [pltpu.VMEM((rows, ff), BF), dma((3, steps))],
            after,
            cost=6.0,
            limit=32,
        )

    def run_mlp_back(layer, source, sums, gate, upward, after):
        last = layer == 1
        outs = far([wide_bf, wide_bf]) + share_outs
        return kernel_call(
            functools.partial(mlp_back, layer, last),
            f"mlp_back_{layer}",
            weights([wg, wu, wd]) + far([gate, upward, *source]) + near(sums),
            outs if last else outs + far([row_bf, line]),
            mlp_scratch + [dma((3, steps))],
            after,
            cost=8.0,
            limit=32,
        )

    def run_attention_back(layer, grad, middle, sums, query, blocks, attn, lse, after):
        return kernel_call(
            functools.partial(attention_back, layer, peers),
            f"attention_back_{layer}",
            weights([wo])
            + far([grad, middle, gains[1][layer], query, bias, attn, lse, cosine, sine, *blocks])
            + near(sums),
            far([row_f32, row_bf, line, head_bf, shape((rows, 2 * kv_width), F32)] + [kv_bf] * (peers - 1)),
            head_scratch
            + [
                pltpu.VMEM((groups, tokens, HEAD_DIM), F32),
                pltpu.VMEM((groups, tokens, HEAD_DIM), F32),
                pltpu.VMEM((q_width, width), BF),
                rows_buf,
                dma,
            ],
            after,
            cost=9.0,
            limit=min(16 + 4 * peers, 56),
        )

    def run_qkv_back(layer, pre_query, pieces, after):
        return kernel_call(
            functools.partial(qkv_back, layer),
            f"qkv_back_{layer}",
            weights([wq, wk, wv]) + far([pre_query, cosine, sine]) + loose(pieces),
            far([kv_bf, kv_bf]) + share_outs,
            qkv_scratch + [total_buf, dma((3,))],
            after,
            cost=4.0,
        )

    def weight_grad(groups, name, direct, after=()):
        ins, tall = [], 0
        for left, left_other, mine, mine_other in groups:
            ins += far([left]) + loose([left_other]) + far([mine]) + loose([mine_other])
            tall += mine.shape[1]
        if not direct:
            tall = -(-tall // 128) * 128
        block = shape((width // peers, tall), BF)
        whole = shape((peers, width // peers, tall), BF)
        blocks = kernel_call(
            functools.partial(grad_blocks, direct),
            name,
            ins,
            far([block] * peers if direct else [whole]),
            [pltpu.VMEM(whole.shape, BF)] if direct else [],
            after,
            cost=8.0,
        )
        if not direct:
            return lax.psum_scatter(blocks[0], "dp", scatter_dimension=0, tiled=False)
        pieces = [blocks[0]]
        for step in range(1, peers):
            pairing = [(peer, peer ^ step) for peer in range(peers)]
            pieces.append(lax.ppermute(blocks[step], "dp", pairing))

        def total():
            return kernel_call(
                add_blocks, "add_" + name, far(pieces[:1]) + loose(pieces[1:]), far([block])
            )[0]

        return total

    def whole_grads(body, name, per_layer, dims):
        kept = pick(per_layer[0], per_layer[1])
        received = swap(pick(per_layer[1], per_layer[0]))
        return kernel_call(
            body, name, loose([kept, received]), far([shape(dim, F32) for dim in dims]), cost=4.0
        )

    def by_layer(per_layer):
        received = swap(pick(per_layer[1], per_layer[0]))
        kept = pick(per_layer[0], per_layer[1])
        return jnp.stack([pick(kept, received), pick(received, kept)])[None]

    hidden = pick(layer_input[0], layer_input[1])
    grad = pick(out_grad[0], out_grad[1])
    saved, outputs = [], []
    grad_other = soon(grad)
    for layer in range(2):
        if layer == 0:
            query, kv, normed_one = run_qkv(layer, hidden, [], [])
        else:
            query, kv, normed_one, hidden = run_qkv(layer, middle, sums, collect())
            outputs.append(hidden)
        blocks = [kv]
        for step in range(1, peers):
            blocks.append(lax.ppermute(kv, "dp", peer_pairs(peers, step, False)))
        early = collect()
        if layer == 0:
            early += raw([other for _, other in pairs])
        normed_one = (normed_one, soon(normed_one))
        *results, attn, lse = (outs := run_attention(layer, query, blocks, early))[:-shares]
        sums = sum_tensor(outs[-shares:])
        early = collect()
        head_halves = (results[0], soon(results[1]))
        middle, normed_two, gate, upward, act_mine, act_theirs, *parts = run_mlp(
            layer, hidden, sums, early
        )
        if layer == 0:
            sums = sum_tensor(parts)
        early = collect()
        act_halves = (act_mine, soon(act_theirs))
        normed_two = (normed_two, soon(normed_two))
        Order.pending += [value for value, _ in early]
        saved.append(
            (hidden, query, blocks, normed_one, head_halves, attn, lse)
            + (middle, normed_two, gate, upward, act_halves)
        )

    last_middle, last_parts = middle, parts
    in_grads, vectors, mlp_totals = [None, None], [None, None], [None, None]
    source, sums = [grad], []
    for layer in (1, 0):
        (hidden, query, blocks, normed_one, head_halves, attn, lse) = saved[layer][:7]
        (middle, normed_two, gate, upward, act_halves) = saved[layer][7:]
        if layer == 1:
            mine, theirs, *parts = run_mlp_back(layer, source, sums, gate, upward, [])
        else:
            mine, theirs, *parts, grad, gain_one = run_mlp_back(
                layer, source, sums, gate, upward, []
            )
            in_grads[1] = grad
        if layer == 0:
            grad_other = soon(grad)
        mlp_groups = [(*normed_two, mine, soon(theirs)), (grad, grad_other, *act_halves)]
        received = spread(parts)
        sums = spread([add_rows(received, collect())] * shares)
        due = []
        if layer == 1:
            last_received = spread(last_parts)
        else:
            mlp_totals[0] = weight_grad(mlp_groups, "grad_mlp_0", False)
            due = []
        middle_grad, low, gain_two, pre_query, *pieces = run_attention_back(
            layer, grad, middle, sums, query, blocks, attn, lse, due
        )
        low_other = soon(low)
        far_pieces = [
            lax.ppermute(pieces[step], "dp", peer_pairs(peers, step, True))
            for step in range(1, peers)
        ]
        if layer == 1:
            last_sums = spread([add_rows(last_received)] * shares)
            mlp_totals[1] = weight_grad(
                mlp_groups, "grad_mlp_1", False, [(far_pieces[0], LOOSE_RAW)]
            )
        else:
            (output,) = kernel_call(
                last_output,
                "last_output",
                far([last_middle]) + near(last_sums),
                far([row_bf]),
                [rows_buf],
                cost=2.0,
            )
            outputs.append(output)
        mine, theirs, *parts = run_qkv_back(
            layer, pre_query, [pieces[0]] + far_pieces, collect() + (raw([mlp_totals[1], head_later]) if layer == 0 else [])
        )
        head_groups = [(low, low_other, *head_halves), (*normed_one, mine, soon(theirs))]
        received = spread(parts)
        if layer == 0:
            head_total = weight_grad(head_groups, "grad_head_0", True)
            sums = spread([add_rows(received, collect())] * shares)
            head_total = head_total()
        else:
            sums = spread([add_rows(received, collect())] * shares)
            head_later = weight_grad(head_groups, "grad_head_1", False)
        source = [middle_grad, hidden, gains[0][layer]]
        vectors[layer] = gain_two
    in_grads[0], last_line = kernel_call(
        finish,
        "finish",
        far(source) + near(sums),
        far([row_bf, line]),
        [rows_buf],
    )
    lines = jnp.concatenate([last_line, vectors[0], gain_one, vectors[1]], axis=0)
    for axis in ("section", "dp"):
        for bit in range((lax.axis_size(axis) - 1).bit_length()):
            pairing = [(peer, peer ^ (1 << bit)) for peer in range(lax.axis_size(axis))]
            lines = lines + lax.ppermute(lines, axis, pairing)

    activations = by_layer(outputs)
    input_grads = by_layer(in_grads)
    size = width // peers
    head_parts = [head_total, head_later[:, : head_total.shape[1]]]
    grad_gate, grad_up, grad_down = whole_grads(
        mlp_grads, "mlp_grads", mlp_totals, [(size, ff), (size, ff), (ff, size)]
    )
    grad_out, grad_query, grad_key, grad_value = whole_grads(
        head_grads,
        "head_grads",
        head_parts,
        [(q_width, size), (size, q_width), (kv_width, size), (kv_width, size)],
    )
    grad_key, grad_value = grad_key.T, grad_value.T
    lines = lax.dynamic_slice_in_dim(lines, me * size, size, 1)
    return (
        activations,
        input_grads,
        pick(lines[0], lines[2])[None],
        grad_query[None],
        grad_key[None],
        grad_value[None],
        grad_out[None],
        pick(lines[1], lines[3])[None],
        grad_gate[None],
        grad_up[None],
        grad_down[None],
    )


def solution(mesh):
    placed = (
        P(None, "dp", None),
        P(),
        P("section", None),
        P("section", None, "tensor"),
        P("section", None, "tensor"),
        P("section", None, "tensor"),
        P("section", "tensor", None),
        P("section", None),
        P("section", None, "tensor"),
        P("section", None, "tensor"),
        P("section", "tensor", None),
        P(None, "dp", None),
    )
    return jax.shard_map(
        per_device,
        mesh=mesh,
        in_specs=placed,
        out_specs=(
            P("section", None, "dp", None),
            P("section", None, "dp", None),
            P("section", "dp"),
            P("section", "dp", "tensor"),
            P("section", "dp", "tensor"),
            P("section", "dp", "tensor"),
            P("section", "tensor", "dp"),
            P("section", "dp"),
            P("section", "dp", "tensor"),
            P("section", "dp", "tensor"),
            P("section", "tensor", "dp"),
        ),
        check_vma=False,
    )
```

```python
import functools

import jax
import jax.numpy as jnp
from jax import lax
from jax.experimental import pallas as pl
from jax.experimental.pallas import tpu as pltpu
from jax.sharding import PartitionSpec as P

HEAD_DIM = 96
EPS = 1e-05
THETA = 100000.0
MASKED = -1e30
BF = jnp.bfloat16
F32 = jnp.float32
FACTOR = HEAD_DIM ** (-0.5)
TILE = 256


def dot(left, right):
    return jnp.dot(left, right, preferred_element_type=F32)


def dot_t(left, right):
    return lax.dot_general(left, right, (((1,), (1,)), ((), ())), preferred_element_type=F32)


def outer(left, right):
    return lax.dot_general(left, right, (((0,), (0,)), ((), ())), preferred_element_type=F32)


def swap(value):
    return lax.ppermute(value, "section", [(0, 1), (1, 0)])


def shape(dims, dtype):
    return jax.ShapeDtypeStruct(dims, dtype)


VMEM = pl.BlockSpec(memory_space=pltpu.VMEM)
ANY = pl.BlockSpec(memory_space=pl.ANY)
NEAR, FAR, RAW, LOOSE, LOOSE_RAW = "near", "far", "raw", "loose", "loose raw"


class Late:
    def __init__(self, source, buffer, sem):
        self.buffer = buffer
        self.copy = pltpu.make_async_copy(source, buffer, sem)
        self.copy.start()
        self.waited = False

    def __getitem__(self, index):
        if not self.waited:
            self.copy.wait()
            self.waited = True
        return self.buffer[index]


class Leaving:
    def __init__(self, buffer, target, sem):
        self.buffer, self.target, self.sem = buffer, target, sem
        self.copy = pltpu.make_async_copy(buffer, target, sem)
        self.started = False

    def __setitem__(self, index, value):
        self.buffer[index] = value

    def __getitem__(self, index):
        return self.buffer[index]

    def send(self, *parts):
        if parts:
            for index in parts:
                pltpu.make_async_copy(self.buffer.at[index], self.target.at[index], self.sem).start()
        elif not self.started:
            self.copy.start()
        self.started = True


def fixed(value, where):
    if where in (LOOSE, LOOSE_RAW):
        return value
    return pltpu.with_memory_space_constraint(value, pltpu.VMEM if where == NEAR else pltpu.HBM)


class Order:
    token = ()
    pending = []


def soon(value):
    other = swap(value)
    Order.pending.append(other)
    return other


def follow(own, value):
    return [(weight, swap(weight)) for weight in lax.optimization_barrier((*own, value))[:-1]]


def collect():
    values, Order.pending = Order.pending, []
    return [(value, LOOSE_RAW) for value in values]


def kernel_call(body, name, ins, outs, scratch=(), after=(), cost=1.0, limit=24):
    after = [*after, *Order.token]
    far_in = [i for i, (_, where) in enumerate(ins) if where in (FAR, LOOSE)]
    far_out = [i for i, (_, where) in enumerate(outs) if where == FAR]
    buffers = [pltpu.VMEM(ins[i][0].shape, ins[i][0].dtype) for i in far_in]
    buffers += [pltpu.VMEM(outs[i][0].shape, outs[i][0].dtype) for i in far_out]
    count = len(far_in) + len(far_out)
    if count:
        buffers.append(pltpu.SemaphoreType.DMA((count,)))

    def whole(*refs):
        refs = list(refs)
        in_refs, refs = refs[: len(ins)], refs[len(ins) + len(after) :]
        out_refs, refs = refs[: len(outs)], refs[len(outs) :]
        own, refs = refs[: len(buffers)], refs[len(buffers) :]
        for place, index in enumerate(far_in):
            in_refs[index] = Late(in_refs[index], own[place], own[-1].at[place])
        for place, index in enumerate(far_out, len(far_in)):
            out_refs[index] = Leaving(own[place], out_refs[index], own[-1].at[place])
        body(in_refs, out_refs, *refs)
        for index in far_in:
            in_refs[index][0:1]
        for index in far_out:
            out_refs[index].send()
        for index in far_out:
            out_refs[index].copy.wait()

    call = pl.pallas_call(
        whole,
        out_shape=[
            pltpu.VMEM(out.shape, out.dtype) if where == NEAR else pltpu.HBM(out.shape, out.dtype)
            for out, where in outs
        ],
        in_specs=[VMEM if where == NEAR else ANY for _, where in ins] + [ANY] * len(after),
        out_specs=[VMEM if where == NEAR else ANY for _, where in outs],
        scratch_shapes=buffers + list(scratch),
        compiler_params=pltpu.CompilerParams(vmem_limit_bytes=limit * 1024 * 1024),
        cost_estimate=pl.CostEstimate(flops=int(cost * 1e9), bytes_accessed=0, transcendentals=0),
        name=name,
    )
    results = call(*[fixed(value, where) for value, where in [*ins, *after]])
    best = min(range(len(outs)), key=lambda index: outs[index][0].size)
    Order.token = ((results[best], NEAR if outs[best][1] == NEAR else RAW),)
    return results


def near(values):
    return [(value, NEAR) for value in values]


def far(values):
    return [(value, FAR) for value in values]


def raw(values):
    return [(value, RAW) for value in values]


def loose(values):
    return [(value, LOOSE) for value in values]


def weights(pairs):
    return raw([weight for pair in pairs for weight in pair])


def fetch(layer, copies):
    mine = lax.axis_index("section") == layer

    @pl.when(mine)
    def _():
        for own, _, buffer, sem in copies:
            pltpu.make_async_copy(own, buffer, sem).start()

    @pl.when(jnp.logical_not(mine))
    def _():
        for _, other, buffer, sem in copies:
            pltpu.make_async_copy(other, buffer, sem).start()


def arrived(own, buffer, sem):
    pltpu.make_async_copy(own, buffer, sem).wait()


def bring_body(layer, groups, ins, outs, sem):
    copies, place = [], 0
    for group, out in zip(groups, outs):
        start = 0
        for _ in range(group):
            own, other = ins[2 * place : 2 * place + 2]
            count = own.shape[1]
            copies.append((own.at[0], other.at[0], out.at[pl.ds(start, count)], sem.at[place]))
            start += count
            place += 1
    if copies:
        fetch(layer, copies)
    rest = [
        pltpu.make_async_copy(source, out, sem.at[index])
        for index, (source, out) in enumerate(zip(ins[2 * place :], outs[len(groups) :]), place)
    ]
    for copy in rest:
        copy.start()
    for own, _, buffer, one in copies:
        arrived(own, buffer, one)
    for copy in rest:
        copy.wait()


def bring(layer, name, groups, values):
    shapes = []
    for group in groups:
        count = sum(own.shape[1] for own, _ in group)
        shapes.append(shape((count, group[0][0].shape[2]), BF))
    shapes += [shape(value.shape, value.dtype) for value in values]
    pairs = [pair for group in groups for pair in group]
    return near(
        kernel_call(
            functools.partial(bring_body, layer, [len(group) for group in groups]),
            name,
            weights(pairs) + raw(values),
            near(shapes),
            [pltpu.SemaphoreType.DMA((len(pairs) + len(values),))],
            cost=2.0,
        )
    )


def share_of(step, size):
    start = lax.bitwise_xor(lax.axis_index("tensor"), step) * size
    return pl.ds(pl.multiple_of(start, size), size)


def summed(refs, buffer):
    for step, ref in enumerate(refs):
        buffer[share_of(step, ref.shape[0]), :] = ref[...]
    return buffer[...].astype(F32)


def store_shares(total, refs):
    size = total.shape[0] // len(refs)
    for step, ref in enumerate(refs):
        ref[...] = total[share_of(step, size), :].astype(BF)


def store_halves(value, mine_out, theirs_out):
    half = value.shape[1] // 2
    early = lax.axis_index("section") == 0
    left, right = value[:, :half], value[:, half:]
    mine_out[...] = jnp.where(early, left, right)
    theirs_out[...] = jnp.where(early, right, left)


def send_half(source, mine_out, theirs_out, place, in_first):
    mine = (lax.axis_index("section") == 0) == in_first
    for chosen, out in ((mine, mine_out), (jnp.logical_not(mine), theirs_out)):

        @pl.when(chosen)
        def _(out=out):
            pltpu.make_async_copy(source, out.target.at[:, place], out.sem).start()

        out.started = True


def norm_scale(values):
    return lax.rsqrt(jnp.mean(values * values, axis=-1, keepdims=True) + EPS)


def norm_back(values, scale, gain, grad):
    weighted = grad * gain
    coupling = jnp.mean(weighted * values, axis=-1, keepdims=True)
    return scale * weighted - values * (scale * scale * scale * coupling)


def rotate(flat, cosine, sine):
    width = flat.shape[1]
    half = HEAD_DIM // 2
    lane = lax.broadcasted_iota(jnp.int32, flat.shape, 1) % HEAD_DIM
    partner = jnp.where(
        lane < half, pltpu.roll(flat, width - half, 1), pltpu.roll(flat, half, 1)
    )
    return flat * cosine + partner * sine


def key_tables(cosine, sine):
    lane = lax.broadcasted_iota(jnp.int32, cosine.shape, 1)
    is_key = lane < cosine.shape[1] // 2
    return jnp.where(is_key, cosine, 1.0), jnp.where(is_key, sine, 0.0)


def qkv_copies(wq, wk, wv, q_buf, kv_buf, sem):
    kv = wk[0].shape[1]
    return [
        (wq[0].at[0], wq[1].at[0], q_buf, sem.at[0]),
        (wk[0].at[0], wk[1].at[0], kv_buf.at[pl.ds(0, kv)], sem.at[1]),
        (wv[0].at[0], wv[1].at[0], kv_buf.at[pl.ds(kv, kv)], sem.at[2]),
    ]


def norm_qkv(layer, first, ins, outs, *scratch):
    gain, cosine, sine = ins[:3]
    query_out, kv_out, normed_out, query_saved = outs[:4]
    copies = []
    if first:
        q_buf, kv_buf, sem = scratch
        copies = qkv_copies(ins[3:5], ins[5:7], ins[7:9], q_buf, kv_buf, sem)
        fetch(layer, copies)
        hidden = ins[9][...].astype(F32)
    else:
        q_buf, kv_buf = ins[3:5]
        low = (ins[5][...].astype(F32) + summed(ins[6:], scratch[0])).astype(BF)
        outs[4][...] = low
        outs[4].send()
        hidden = low.astype(F32)
    normed = (hidden * norm_scale(hidden) * gain[...]).astype(BF)
    normed_out[...] = normed
    normed_out.send()
    cos, sin = cosine[...], sine[...]
    key_cos, key_sin = key_tables(cos, sin)
    for own, _, buffer, one in copies:
        arrived(own, buffer, one)
    query = rotate(dot(normed, q_buf[...]), cos, sin).astype(BF)
    query_saved[...] = query
    query_saved.send()
    query_out[...] = query
    kv_out[...] = rotate(dot_t(normed, kv_buf[...]), key_cos, key_sin).astype(BF)


def split_keys(kv_refs, k_buf, v_buf):
    groups = k_buf.shape[0]
    rows = k_buf.shape[1] // len(kv_refs)
    for index, ref in enumerate(kv_refs):
        block = ref[...]
        for group in range(groups):
            low = group * HEAD_DIM
            k_buf[group, index * rows : (index + 1) * rows, :] = block[:, low : low + HEAD_DIM]
            low = (groups + group) * HEAD_DIM
            v_buf[group, index * rows : (index + 1) * rows, :] = block[:, low : low + HEAD_DIM]


def attention(ins, outs, q_buf, sum_buf):
    wo_buf, bias, query = ins[:3]
    kv_refs = ins[3:]
    mine_out, theirs_out, attn_out, lse_out, k_buf, v_buf = outs[:6]
    heads = q_buf.shape[0]
    group_size = heads // k_buf.buffer.shape[0]
    split_query(query[...], q_buf)
    split_keys(kv_refs, k_buf.buffer, v_buf.buffer)
    k_buf.send()
    v_buf.send()
    results, totals = [], []
    for head in range(heads):
        group = head // group_size
        scores = dot_t(q_buf[head], k_buf[group]) * FACTOR + bias[...]
        top = jnp.max(scores, axis=-1, keepdims=True)
        weights = jnp.exp(scores - top)
        total = jnp.sum(weights, axis=-1, keepdims=True)
        totals.append(top + jnp.log(total))
        chances = (weights * (1.0 / total)).astype(BF)
        results.append(dot(chances, v_buf[group]))
    attn = jnp.concatenate(results, axis=1)
    attn_out[...] = attn
    attn_out.send()
    lse_out[...] = jnp.concatenate(totals, axis=1)
    rows = attn.astype(BF)
    store_halves(rows, mine_out, theirs_out)
    sum_buf[...] = dot(rows, wo_buf[...])
    store_shares(sum_buf, outs[6:])


def split_query(query, q_buf):
    for head in range(q_buf.shape[0]):
        q_buf[head] = query[:, head * HEAD_DIM : (head + 1) * HEAD_DIM]


def mlp(ins, outs, total, rows_buf, act_buf):
    wg, wu, wd, hidden, gain = ins[:5]
    middle_out, normed_out, gate_out, up_out, mine_out, theirs_out = outs[:6]
    middle = hidden[...].astype(F32) + summed(ins[5:], rows_buf)
    middle_out[...] = middle.astype(BF)
    middle_out.send()
    normed_out[...] = (middle * norm_scale(middle) * gain[...]).astype(BF)
    normed_out.send()
    for step in range(wg.shape[1] // TILE):
        part = slice(step * TILE, (step + 1) * TILE)
        gate = dot(normed_out[...], wg[:, part])
        upward = dot(normed_out[...], wu[:, part])
        gate_out[:, part] = gate.astype(BF)
        up_out[:, part] = upward.astype(BF)
        act = (gate * jax.nn.sigmoid(gate) * upward).astype(BF)
        gate_out.send((slice(None), part))
        up_out.send((slice(None), part))
        act_buf[:, part] = act
        half = act_buf.shape[1] // 2
        place = slice(step * TILE % half, step * TILE % half + TILE)
        send_half(act_buf.at[:, part], mine_out, theirs_out, place, step * TILE < half)
        term = dot(act, wd[part, :])
        if step == 0:
            total[...] = term
        else:
            total[...] += term
    store_shares(total, outs[6:])


def mlp_back(last, ins, outs, total, rows_buf):
    wg, wu, wd, gate_ref, up_ref = ins[:5]
    mine_out, theirs_out = outs[:2]
    shares = outs[2:] if last else outs[2:-2]
    early = lax.axis_index("section") == 0
    if last:
        grad_ref = ins[5]
    else:
        middle_grad, hidden, gain = ins[5:8]
        grad_ref, gain_out = outs[-2:]
        values, grad = hidden[...].astype(F32), summed(ins[8:], rows_buf)
        scale = norm_scale(values)
        gain_out[...] = jnp.sum(grad * values * scale, axis=0, keepdims=True)
        grad_ref[...] = (middle_grad[...].astype(F32) + norm_back(values, scale, gain[...], grad)).astype(BF)
        grad_ref.send()
    for step in range(wg.shape[1] // TILE):
        part = slice(step * TILE, (step + 1) * TILE)
        act_grad = dot_t(grad_ref[...], wd[part, :])
        gate, upward = gate_ref[:, part].astype(F32), up_ref[:, part].astype(F32)
        sigma = jax.nn.sigmoid(gate)
        gate_grad = (act_grad * upward * sigma * (1.0 + gate * (1.0 - sigma))).astype(BF)
        up_grad = (act_grad * gate * sigma).astype(BF)
        mine_out[:, part] = jnp.where(early, gate_grad, up_grad)
        theirs_out[:, part] = jnp.where(early, up_grad, gate_grad)
        theirs_out.send((slice(None), part))
        mine_out.send((slice(None), part))
        term = dot_t(gate_grad, wg[:, part]) + dot_t(up_grad, wu[:, part])
        if step == 0:
            total[...] = term
        else:
            total[...] += term
    store_shares(total, shares)


def attention_back(peers, ins, outs, q_buf, dk_buf, dv_buf, rows_buf):
    wo_buf, grad_in, middle, gain, query, bias, attn, lse, cosine, sine, k_buf, v_buf = ins[:12]
    sums = ins[12:]
    low_out, gain_out, pre_out = outs[:3]
    block_outs = outs[3:]
    heads, groups = q_buf.shape[0], k_buf.shape[0]
    group_size = heads // groups
    grad = summed(sums, rows_buf)
    values = middle[...].astype(F32)
    scale = norm_scale(values)
    gain_out[...] = jnp.sum(grad * values * scale, axis=0, keepdims=True)
    middle_grad = grad_in[...].astype(F32) + norm_back(values, scale, gain[...], grad)
    low_out[...] = middle_grad.astype(BF)
    low_out.send()
    attn_grad = dot_t(low_out[...], wo_buf[...]).astype(BF)
    split_query(query[...], q_buf)
    query_grads = []
    for head in range(heads):
        group = head // group_size
        lanes = slice(head * HEAD_DIM, (head + 1) * HEAD_DIM)
        head_grad = attn_grad[:, lanes]
        delta = jnp.sum(head_grad.astype(F32) * attn[:, lanes], axis=-1, keepdims=True)
        scores = dot_t(q_buf[head], k_buf[group]) * FACTOR + bias[...]
        chances = jnp.exp(scores - lse[:, head : head + 1])
        chance_grad = dot_t(head_grad, v_buf[group])
        score_grad = (chances * (chance_grad - delta) * FACTOR).astype(BF)
        query_grads.append(dot(score_grad, k_buf[group]))
        key_term = outer(score_grad, q_buf[head])
        value_term = outer(chances.astype(BF), head_grad)
        if head % group_size == 0:
            dk_buf[group] = key_term
            dv_buf[group] = value_term
        else:
            dk_buf[group] += key_term
            dv_buf[group] += value_term
    rows = middle_grad.shape[0]
    for index in reversed(range(peers)):
        span = slice(index * rows, (index + 1) * rows)
        block = jnp.concatenate(
            [dk_buf[group, span, :] for group in range(groups)]
            + [dv_buf[group, span, :] for group in range(groups)],
            axis=1,
        )
        block_outs[index][...] = block if index == 0 else block.astype(BF)
        block_outs[index].send()
    query_grad = jnp.concatenate(query_grads, axis=1)
    pre_out[...] = rotate(query_grad, cosine[...], -sine[...]).astype(BF)


def qkv_back(ins, outs, total):
    q_buf, kv_buf, cosine, sine, pre_query, own = ins[:6]
    mine_out, theirs_out = outs[:2]
    both = own[...]
    for ref in ins[6:]:
        both = both + ref[...].astype(F32)
    key_cos, key_sin = key_tables(cosine[...], sine[...])
    pre = rotate(both, key_cos, -key_sin).astype(BF)
    early = lax.axis_index("section") == 0
    pre_q = pre_query[...]
    mine_out[...] = jnp.where(early, pre_q, pre)
    theirs_out[...] = jnp.where(early, pre, pre_q)
    theirs_out.send()
    mine_out.send()
    total[...] = dot_t(pre_q, q_buf[...]) + dot(pre, kv_buf[...])
    store_shares(total, outs[2:])


def last_output(ins, outs, rows_buf):
    outs[0][...] = (ins[0][...].astype(F32) + summed(ins[1:], rows_buf)).astype(BF)


def finish(ins, outs, rows_buf):
    middle_grad, hidden, gain = ins[:3]
    values, grad = hidden[...].astype(F32), summed(ins[3:], rows_buf)
    scale = norm_scale(values)
    outs[0][...] = (middle_grad[...].astype(F32) + norm_back(values, scale, gain[...], grad)).astype(BF)
    outs[0].send()
    outs[1][...] = jnp.sum(grad * values * scale, axis=0, keepdims=True)


def grad_blocks(spread, ins, outs, *scratch):
    buffer = scratch[0] if spread else outs[0].buffer
    peers = len(outs) if spread else outs[0].buffer.shape[0]
    me = lax.axis_index("dp")
    start = 0
    for left, left_other, right, right_other in zip(*[iter(ins)] * 4):
        wide, wide_other = right[...], right_other[...]
        size = left.buffer.shape[1] // peers
        lanes = slice(start, start + wide.shape[1])
        for block in range(peers):
            span = slice(block * size, (block + 1) * size)
            term = outer(left[:, span], wide) + outer(left_other[:, span], wide_other)
            place = lax.bitwise_xor(me, block) if spread else block
            buffer[place, :, lanes] = term.astype(BF)
        start += wide.shape[1]
    if start < buffer.shape[-1]:
        rest = buffer.shape[-1] - start
        buffer[:, :, start:] = jnp.zeros((peers, buffer.shape[1], rest), BF)
    if spread:
        for index, out in enumerate(outs):
            out[...] = buffer[index]
            out.send()


def add_blocks(ins, outs):
    total = ins[0][...].astype(F32)
    for block in ins[1:]:
        total = total + block[...].astype(F32)
    outs[0][...] = total.astype(BF)


def grad_parts(kept, received):
    early = lax.axis_index("section") == 0

    def halves(lanes):
        own, other = kept[:, lanes].astype(F32), received[:, lanes].astype(F32)
        return jnp.where(early, own, other), jnp.where(early, other, own)

    return halves


def mlp_grads(ins, outs):
    halves = grad_parts(*ins)
    gate_out, up_out, down_out = outs
    ff = gate_out.buffer.shape[1]
    gate, upward = halves(slice(0, ff))
    gate_out[...] = gate
    gate_out.send()
    up_out[...] = upward
    up_out.send()
    half = ff // 2
    for index, part in enumerate(halves(slice(ff, ff + half))):
        down_out[index * half : (index + 1) * half, :] = part.T


def head_grads(ins, outs):
    halves = grad_parts(*ins)
    out_out, query_out, key_out, value_out = outs
    half = out_out.buffer.shape[0] // 2
    for index, part in enumerate(halves(slice(0, half))):
        out_out[index * half : (index + 1) * half, :] = part.T
    query, key_value = halves(slice(half, 3 * half))
    query_out[...] = query
    flipped = key_value.T
    key_out[...] = flipped[:half]
    value_out[...] = flipped[half:]


def add_shares(ins, outs):
    total = ins[0][...].astype(F32)
    for ref in ins[1:]:
        total = total + ref[...].astype(F32)
    outs[0][...] = total.astype(BF)


def spread(values):
    peers = len(values)
    return [values[0]] + [
        lax.ppermute(values[step], "tensor", [(peer, peer ^ step) for peer in range(peers)])
        for step in range(1, peers)
    ]


def add_rows(received, after=()):
    (total,) = kernel_call(
        add_shares,
        "add_shares",
        near(received),
        near([shape(received[0].shape, BF)]),
        after=after,
        cost=0.5,
    )
    return total


def sum_tensor(parts):
    return spread([add_rows(spread(parts))] * len(parts))


def layout(lengths, token_count):
    seq_ends = jnp.cumsum(lengths)
    starts = seq_ends - lengths
    places = jnp.arange(token_count, dtype=jnp.int32)
    segment = jnp.sum((places[:, None] >= seq_ends[None, :]).astype(jnp.int32), axis=1)
    labels = jnp.arange(lengths.shape[0], dtype=jnp.int32)
    offset = jnp.sum(jnp.where(segment[:, None] == labels[None, :], starts[None, :], 0), axis=1)
    return (segment, places - offset)


def rope_tables(position, heads):
    halfway = HEAD_DIM // 2
    inverse = THETA ** (-2.0 * jnp.arange(halfway, dtype=F32) / HEAD_DIM)
    angles = position.astype(F32)[:, None] * inverse[None, :]
    cosine, sine = jnp.cos(angles), jnp.sin(angles)
    return (
        jnp.tile(jnp.concatenate([cosine, cosine], axis=-1), (1, heads)),
        jnp.tile(jnp.concatenate([-sine, sine], axis=-1), (1, heads)),
    )


def peer_pairs(peers, step, later):
    pairs = [(low, low ^ step) for low in range(peers) if low < low ^ step]
    return [(high, low) for low, high in pairs] if later else pairs


def per_device(
    layer_input,
    seq_lengths,
    norm1_gain,
    w_query,
    w_key,
    w_value,
    w_out,
    norm2_gain,
    w_gate,
    w_up,
    w_down,
    out_grad,
):
    Order.token, Order.pending = (), []
    rows, width = layer_input.shape[1:]
    peers = lax.axis_size("dp")
    me = lax.axis_index("dp")
    first = lax.axis_index("section") == 0
    q_width, kv_width, ff = w_query.shape[2], w_key.shape[2], w_gate.shape[2]
    heads, groups = q_width // HEAD_DIM, kv_width // HEAD_DIM
    tokens = rows * peers
    shares = lax.axis_size("tensor")

    def pick(early, late):
        return jnp.where(first, early, late)

    own = [w_query, jnp.swapaxes(w_key, 1, 2), jnp.swapaxes(w_value, 1, 2), w_out, w_gate, w_up, w_down]
    wq, wk, wv = [(weight, swap(weight)) for weight in own[:3]]
    gains = []
    for gain in (norm1_gain, norm2_gain):
        other = swap(gain)
        gains.append((pick(gain, other), pick(other, gain)))

    segment, position = layout(pick(seq_lengths[0], seq_lengths[1]), tokens)
    row_seg = lax.dynamic_slice_in_dim(segment, me * rows, rows, 0)
    row_pos = lax.dynamic_slice_in_dim(position, me * rows, rows, 0)
    local = jnp.arange(rows, dtype=jnp.int32)
    key_place = jnp.concatenate([(me ^ step) * rows + local for step in range(peers)])
    key_seg = jnp.concatenate(
        [lax.dynamic_slice_in_dim(segment, (me ^ step) * rows, rows, 0) for step in range(peers)]
    )
    allowed = (row_seg[:, None] == key_seg[None, :]) & (
        key_place[None, :] <= (me * rows + local)[:, None]
    )
    bias = jnp.where(allowed, 0.0, MASKED).astype(F32)
    cosine, sine = rope_tables(row_pos, heads)

    share = shape((rows // shares, width), BF)
    share_outs = near([share] * shares)
    rows_buf = pltpu.VMEM((rows, width), BF)
    total_buf = pltpu.VMEM((rows, width), F32)
    row_f32 = shape((rows, width), F32)
    row_bf = shape((rows, width), BF)
    line = shape((1, width), F32)
    head_bf = shape((rows, q_width), BF)
    half_head = shape((rows, q_width // 2), BF)
    half_wide = shape((rows, ff // 2), BF)
    kv_bf = shape((rows, 2 * kv_width), BF)
    wide_f32 = shape((rows, ff), F32)
    wide_bf = shape((rows, ff), BF)
    dma = pltpu.SemaphoreType.DMA
    qkv_scratch = [
        pltpu.VMEM((width, q_width), BF),
        pltpu.VMEM((2 * kv_width, width), BF),
    ]
    mlp_scratch = [total_buf, rows_buf]
    keys_bf = shape((groups, tokens, HEAD_DIM), BF)
    head_scratch = [pltpu.VMEM((heads, rows, HEAD_DIM), BF)]

    def run_qkv(layer, ins, after):
        start = layer == 0
        outs = near([head_bf, kv_bf]) + far([row_bf, head_bf])
        return kernel_call(
            functools.partial(norm_qkv, layer, start),
            f"norm_qkv_{layer}",
            ins,
            outs if start else outs + far([row_bf]),
            qkv_scratch + [dma((3,))] if start else [rows_buf],
            after,
            cost=4.0,
        )

    def run_attention(layer, brought, query, blocks, after):
        outs = [half_head] * 2 + [shape((rows, q_width), F32), shape((rows, heads), F32)] + [keys_bf] * 2
        return kernel_call(
            attention,
            f"attention_{layer}",
            brought + near([query, *blocks]),
            far(outs) + share_outs,
            head_scratch + [total_buf],
            after,
            cost=5.0,
            limit=min(8 + 4 * peers, 28),
        )

    def run_mlp(layer, brought, sums, after):
        return kernel_call(
            mlp,
            f"mlp_{layer}",
            brought + near(sums),
            far([row_bf, row_bf, wide_bf, wide_bf, half_wide, half_wide])
            + (share_outs if layer == 0 else far([share] * shares)),
            mlp_scratch + [pltpu.VMEM((rows, ff), BF)],
            after,
            cost=6.0,
            limit=24,
        )

    def run_mlp_back(layer, brought, sums, after):
        last = layer == 1
        outs = far([wide_bf, wide_bf]) + share_outs
        return kernel_call(
            functools.partial(mlp_back, last),
            f"mlp_back_{layer}",
            brought + near(sums),
            outs if last else outs + far([row_bf, line]),
            mlp_scratch,
            after,
            cost=8.0,
            limit=24,
        )

    def run_attention_back(layer, brought, sums, after):
        return kernel_call(
            functools.partial(attention_back, peers),
            f"attention_back_{layer}",
            brought + near(sums),
            far([row_bf, line, head_bf, shape((rows, 2 * kv_width), F32)] + [kv_bf] * (peers - 1)),
            head_scratch
            + [
                pltpu.VMEM((groups, tokens, HEAD_DIM), F32),
                pltpu.VMEM((groups, tokens, HEAD_DIM), F32),
                rows_buf,
            ],
            after,
            cost=9.0,
            limit=min(8 + 4 * peers, 40),
        )

    def run_qkv_back(layer, brought, pieces, after):
        return kernel_call(
            qkv_back,
            f"qkv_back_{layer}",
            brought + loose(pieces),
            far([kv_bf, kv_bf]) + share_outs,
            [total_buf],
            after,
            cost=4.0,
        )

    def weight_grad(groups, name, direct, after=()):
        ins, tall = [], 0
        for left, left_other, mine, mine_other in groups:
            ins += far([left]) + loose([left_other]) + far([mine]) + loose([mine_other])
            tall += mine.shape[1]
        if not direct:
            tall = -(-tall // 128) * 128
        block = shape((width // peers, tall), BF)
        whole = shape((peers, width // peers, tall), BF)
        blocks = kernel_call(
            functools.partial(grad_blocks, direct),
            name,
            ins,
            far([block] * peers if direct else [whole]),
            [pltpu.VMEM(whole.shape, BF)] if direct else [],
            after,
            cost=8.0,
        )
        if not direct:
            return lax.psum_scatter(blocks[0], "dp", scatter_dimension=0, tiled=False)
        pieces = [blocks[0]]
        for step in range(1, peers):
            pairing = [(peer, peer ^ step) for peer in range(peers)]
            pieces.append(lax.ppermute(blocks[step], "dp", pairing))

        def total():
            return kernel_call(
                add_blocks, "add_" + name, far(pieces[:1]) + loose(pieces[1:]), far([block])
            )[0]

        return total

    def whole_grads(body, name, per_layer, dims):
        kept = pick(per_layer[0], per_layer[1])
        received = swap(pick(per_layer[1], per_layer[0]))
        return kernel_call(
            body, name, loose([kept, received]), far([shape(dim, F32) for dim in dims]), cost=4.0
        )

    def by_layer(per_layer):
        received = swap(pick(per_layer[1], per_layer[0]))
        kept = pick(per_layer[0], per_layer[1])
        return jnp.stack([pick(kept, received), pick(received, kept)])[None]

    hidden = pick(layer_input[0], layer_input[1])
    grad = pick(out_grad[0], out_grad[1])
    saved, outputs = [], []
    for layer in range(2):
        if layer == 0:
            ins = far([gains[0][layer], cosine, sine]) + weights([wq, wk, wv]) + far([hidden])
            query, kv, normed_one, query_saved = run_qkv(layer, ins, [])
        else:
            ins = ready[2:5] + ready[:2] + ready[5:] + near(sums)
            query, kv, normed_one, query_saved, hidden = run_qkv(layer, ins, collect())
            outputs.append(hidden)
        if layer == 0:
            wo, wg = follow(own[3:5], normed_one)
        blocks = [kv]
        for step in range(1, peers):
            blocks.append(lax.ppermute(kv, "dp", peer_pairs(peers, step, False)))
        early = collect()
        if layer == 0:
            early += raw([wg[1]])
        else:
            grad_other = soon(grad)
            early += collect()
        ready = bring(layer, f"bring_attention_{layer}", [[wo]], [bias])
        *results, attn, lse, keys, values = (outs := run_attention(layer, ready, query, blocks, early))[:-shares]
        received = spread(outs[-shares:])
        if layer == 0:
            wu, wd = follow(own[5:], results[1])
            total = add_rows(received, raw([wu[1], wd[1]]))
        else:
            total = add_rows(received)
        swapped, theirs, _ = lax.optimization_barrier((normed_one, results[1], total))
        normed_one = (normed_one, soon(swapped))
        head_halves = (results[0], soon(theirs))
        sums = spread([total] * shares)
        ready = bring(layer, f"bring_mlp_{layer}", [[wg], [wu], [wd]], [hidden, gains[1][layer]])
        early = collect()
        middle, normed_two, gate, upward, act_mine, act_theirs, *parts = run_mlp(
            layer, ready, sums, early
        )
        if layer == 0:
            sums = sum_tensor(parts)
            ready = bring(
                1, "bring_qkv_1", [[wq], [wk, wv]], [gains[0][1], cosine, sine, middle]
            )
        early = collect()
        act_halves = (act_mine, soon(act_theirs))
        normed_two = (normed_two, soon(normed_two))
        Order.pending += [value for value, _ in early]
        saved.append(
            (hidden, query_saved, (keys, values), normed_one, head_halves, attn, lse)
            + (middle, normed_two, gate, upward, act_halves)
        )

    last_middle, last_parts = middle, parts
    in_grads, vectors, mlp_totals = [None, None], [None, None], [None, None]
    source, sums = [grad], []
    for layer in (1, 0):
        (hidden, query, blocks, normed_one, head_halves, attn, lse) = saved[layer][:7]
        (middle, normed_two, gate, upward, act_halves) = saved[layer][7:]
        if layer == 1:
            mine, theirs, *parts = run_mlp_back(layer, ready[:3] + far([gate, upward, grad]), [], [])
        else:
            mine, theirs, *parts, grad, gain_one = run_mlp_back(
                layer, ready + far([gate, upward, *source]), sums, []
            )
            in_grads[1] = grad
        if layer == 0:
            grad_other = soon(grad)
        mlp_groups = [(*normed_two, mine, soon(theirs)), (grad, grad_other, *act_halves)]
        received = spread(parts)
        sums = spread([add_rows(received, collect())] * shares)
        due = []
        if layer == 1:
            last_received = spread(last_parts)
        else:
            mlp_totals[0] = weight_grad(mlp_groups, "grad_mlp_0", False)
            due = []
        brought = bring(
            layer,
            f"bring_attention_back_{layer}",
            [[wo]],
            [grad, middle, gains[1][layer], query, bias, attn, lse, cosine, sine, *blocks],
        )
        low, gain_two, pre_query, *pieces = run_attention_back(layer, brought, sums, due)
        low_other = soon(low)
        far_pieces = [
            lax.ppermute(pieces[step], "dp", peer_pairs(peers, step, True))
            for step in range(1, peers)
        ]
        if layer == 1:
            last_sums = spread([add_rows(last_received)] * shares)
            mlp_totals[1] = weight_grad(
                mlp_groups, "grad_mlp_1", False, [(far_pieces[0], LOOSE_RAW)]
            )
        else:
            (output,) = kernel_call(
                last_output,
                "last_output",
                far([last_middle]) + near(last_sums),
                far([row_bf]),
                [rows_buf],
                cost=2.0,
            )
            outputs.append(output)
        ready = bring(
            layer,
            f"bring_qkv_back_{layer}",
            [[wq], [wk, wv]],
            [cosine, sine, pre_query, pieces[0]],
        )
        mine, theirs, *parts = run_qkv_back(
            layer, ready, far_pieces, collect() + (raw([mlp_totals[1], head_later]) if layer == 0 else [])
        )
        head_groups = [(low, low_other, *head_halves), (*normed_one, mine, soon(theirs))]
        received = spread(parts)
        if layer == 0:
            head_total = weight_grad(head_groups, "grad_head_0", True)
            sums = spread([add_rows(received, collect())] * shares)
            head_total = head_total()
        else:
            sums = spread([add_rows(received, collect())] * shares)
            head_later = weight_grad(head_groups, "grad_head_1", False)
            ready = bring(0, "bring_mlp_back_0", [[wg], [wu], [wd]], [])
        source = [low, hidden, gains[0][layer]]
        vectors[layer] = gain_two
    in_grads[0], last_line = kernel_call(
        finish,
        "finish",
        bring(0, "bring_finish", [], source) + near(sums),
        far([row_bf, line]),
        [rows_buf],
    )
    lines = jnp.concatenate([last_line, vectors[0], gain_one, vectors[1]], axis=0)
    for axis in ("section", "dp"):
        for bit in range((lax.axis_size(axis) - 1).bit_length()):
            pairing = [(peer, peer ^ (1 << bit)) for peer in range(lax.axis_size(axis))]
            lines = lines + lax.ppermute(lines, axis, pairing)

    activations = by_layer(outputs)
    input_grads = by_layer(in_grads)
    size = width // peers
    head_parts = [head_total, head_later[:, : head_total.shape[1]]]
    grad_gate, grad_up, grad_down = whole_grads(
        mlp_grads, "mlp_grads", mlp_totals, [(size, ff), (size, ff), (ff, size)]
    )
    grad_out, grad_query, grad_key, grad_value = whole_grads(
        head_grads,
        "head_grads",
        head_parts,
        [(q_width, size), (size, q_width), (kv_width, size), (kv_width, size)],
    )
    grad_key, grad_value = grad_key.T, grad_value.T
    lines = lax.dynamic_slice_in_dim(lines, me * size, size, 1)
    return (
        activations,
        input_grads,
        pick(lines[0], lines[2])[None],
        grad_query[None],
        grad_key[None],
        grad_value[None],
        grad_out[None],
        pick(lines[1], lines[3])[None],
        grad_gate[None],
        grad_up[None],
        grad_down[None],
    )


def solution(mesh):
    placed = (
        P(None, "dp", None),
        P(),
        P("section", None),
        P("section", None, "tensor"),
        P("section", None, "tensor"),
        P("section", None, "tensor"),
        P("section", "tensor", None),
        P("section", None),
        P("section", None, "tensor"),
        P("section", None, "tensor"),
        P("section", "tensor", None),
        P(None, "dp", None),
    )
    return jax.shard_map(
        per_device,
        mesh=mesh,
        in_specs=placed,
        out_specs=(
            P("section", None, "dp", None),
            P("section", None, "dp", None),
            P("section", "dp"),
            P("section", "dp", "tensor"),
            P("section", "dp", "tensor"),
            P("section", "dp", "tensor"),
            P("section", "tensor", "dp"),
            P("section", "dp"),
            P("section", "dp", "tensor"),
            P("section", "dp", "tensor"),
            P("section", "tensor", "dp"),
        ),
        check_vma=False,
    )
```

```python
import functools

import jax
import jax.numpy as jnp
from jax import lax
from jax.experimental import pallas as pl
from jax.experimental.pallas import tpu as pltpu
from jax.sharding import PartitionSpec as P

HEAD_DIM = 96
EPS = 1e-05
THETA = 100000.0
MASKED = -1e30
BF = jnp.bfloat16
F32 = jnp.float32
FACTOR = HEAD_DIM ** (-0.5)
TILE = 256


def dot(left, right):
    return jnp.dot(left, right, preferred_element_type=F32)


def dot_t(left, right):
    return lax.dot_general(left, right, (((1,), (1,)), ((), ())), preferred_element_type=F32)


def outer(left, right):
    return lax.dot_general(left, right, (((0,), (0,)), ((), ())), preferred_element_type=F32)


def swap(value):
    return lax.ppermute(value, "section", [(0, 1), (1, 0)])


def shape(dims, dtype):
    return jax.ShapeDtypeStruct(dims, dtype)


VMEM = pl.BlockSpec(memory_space=pltpu.VMEM)
ANY = pl.BlockSpec(memory_space=pl.ANY)
NEAR, FAR, RAW, LOOSE, LOOSE_RAW = "near", "far", "raw", "loose", "loose raw"


class Late:
    def __init__(self, source, buffer, sem):
        self.buffer = buffer
        self.copy = pltpu.make_async_copy(source, buffer, sem)
        self.copy.start()
        self.waited = False

    def __getitem__(self, index):
        if not self.waited:
            self.copy.wait()
            self.waited = True
        return self.buffer[index]


class Leaving:
    def __init__(self, buffer, target, sem):
        self.buffer, self.target, self.sem = buffer, target, sem
        self.copy = pltpu.make_async_copy(buffer, target, sem)
        self.started = False

    def __setitem__(self, index, value):
        self.buffer[index] = value

    def __getitem__(self, index):
        return self.buffer[index]

    def send(self, *parts):
        if parts:
            for index in parts:
                pltpu.make_async_copy(self.buffer.at[index], self.target.at[index], self.sem).start()
        elif not self.started:
            self.copy.start()
        self.started = True


def fixed(value, where):
    if where in (LOOSE, LOOSE_RAW):
        return value
    return pltpu.with_memory_space_constraint(value, pltpu.VMEM if where == NEAR else pltpu.HBM)


class Order:
    token = ()
    pending = []


def soon(value):
    other = swap(value)
    Order.pending.append(other)
    return other


def follow(own, value):
    return [(weight, swap(weight)) for weight in lax.optimization_barrier((*own, value))[:-1]]


def collect():
    values, Order.pending = Order.pending, []
    return [(value, LOOSE_RAW) for value in values]


def kernel_call(body, name, ins, outs, scratch=(), after=(), cost=1.0, limit=24):
    after = [*after, *Order.token]
    far_in = [i for i, (_, where) in enumerate(ins) if where in (FAR, LOOSE)]
    far_out = [i for i, (_, where) in enumerate(outs) if where == FAR]
    buffers = [pltpu.VMEM(ins[i][0].shape, ins[i][0].dtype) for i in far_in]
    buffers += [pltpu.VMEM(outs[i][0].shape, outs[i][0].dtype) for i in far_out]
    count = len(far_in) + len(far_out)
    if count:
        buffers.append(pltpu.SemaphoreType.DMA((count,)))

    def whole(*refs):
        refs = list(refs)
        in_refs, refs = refs[: len(ins)], refs[len(ins) + len(after) :]
        out_refs, refs = refs[: len(outs)], refs[len(outs) :]
        own, refs = refs[: len(buffers)], refs[len(buffers) :]
        for place, index in enumerate(far_in):
            in_refs[index] = Late(in_refs[index], own[place], own[-1].at[place])
        for place, index in enumerate(far_out, len(far_in)):
            out_refs[index] = Leaving(own[place], out_refs[index], own[-1].at[place])
        body(in_refs, out_refs, *refs)
        for index in far_in:
            in_refs[index][0:1]
        for index in far_out:
            out_refs[index].send()
        for index in far_out:
            out_refs[index].copy.wait()

    call = pl.pallas_call(
        whole,
        out_shape=[
            pltpu.VMEM(out.shape, out.dtype) if where == NEAR else pltpu.HBM(out.shape, out.dtype)
            for out, where in outs
        ],
        in_specs=[VMEM if where == NEAR else ANY for _, where in ins] + [ANY] * len(after),
        out_specs=[VMEM if where == NEAR else ANY for _, where in outs],
        scratch_shapes=buffers + list(scratch),
        compiler_params=pltpu.CompilerParams(vmem_limit_bytes=limit * 1024 * 1024),
        cost_estimate=pl.CostEstimate(flops=int(cost * 1e9), bytes_accessed=0, transcendentals=0),
        name=name,
    )
    results = call(*[fixed(value, where) for value, where in [*ins, *after]])
    best = min(range(len(outs)), key=lambda index: outs[index][0].size)
    Order.token = ((results[best], NEAR if outs[best][1] == NEAR else RAW),)
    return results


def near(values):
    return [(value, NEAR) for value in values]


def far(values):
    return [(value, FAR) for value in values]


def raw(values):
    return [(value, RAW) for value in values]


def loose(values):
    return [(value, LOOSE) for value in values]


def weights(pairs):
    return raw([weight for pair in pairs for weight in pair])


def fetch(layer, copies):
    mine = lax.axis_index("section") == layer

    @pl.when(mine)
    def _():
        for own, _, buffer, sem in copies:
            pltpu.make_async_copy(own, buffer, sem).start()

    @pl.when(jnp.logical_not(mine))
    def _():
        for _, other, buffer, sem in copies:
            pltpu.make_async_copy(other, buffer, sem).start()


def arrived(own, buffer, sem):
    pltpu.make_async_copy(own, buffer, sem).wait()


def bring_body(layer, groups, ins, outs, sem):
    copies, place = [], 0
    for group, out in zip(groups, outs):
        start = 0
        for _ in range(group):
            own, other = ins[2 * place : 2 * place + 2]
            count = own.shape[1]
            copies.append((own.at[0], other.at[0], out.at[pl.ds(start, count)], sem.at[place]))
            start += count
            place += 1
    if copies:
        fetch(layer, copies)
    rest = [
        pltpu.make_async_copy(source, out, sem.at[index])
        for index, (source, out) in enumerate(zip(ins[2 * place :], outs[len(groups) :]), place)
    ]
    for copy in rest:
        copy.start()
    for own, _, buffer, one in copies:
        arrived(own, buffer, one)
    for copy in rest:
        copy.wait()


def bring(layer, name, groups, values):
    shapes = []
    for group in groups:
        count = sum(own.shape[1] for own, _ in group)
        shapes.append(shape((count, group[0][0].shape[2]), BF))
    shapes += [shape(value.shape, value.dtype) for value in values]
    pairs = [pair for group in groups for pair in group]
    return near(
        kernel_call(
            functools.partial(bring_body, layer, [len(group) for group in groups]),
            name,
            weights(pairs) + raw(values),
            near(shapes),
            [pltpu.SemaphoreType.DMA((len(pairs) + len(values),))],
            cost=2.0,
        )
    )


def share_of(step, size):
    start = lax.bitwise_xor(lax.axis_index("tensor"), step) * size
    return pl.ds(pl.multiple_of(start, size), size)


def summed(refs, buffer):
    for step, ref in enumerate(refs):
        buffer[share_of(step, ref.shape[0]), :] = ref[...]
    return buffer[...].astype(F32)


def store_shares(total, refs):
    size = total.shape[0] // len(refs)
    for step, ref in enumerate(refs):
        ref[...] = total[share_of(step, size), :].astype(BF)


def store_halves(value, mine_out, theirs_out):
    half = value.shape[1] // 2
    early = lax.axis_index("section") == 0
    left, right = value[:, :half], value[:, half:]
    mine_out[...] = jnp.where(early, left, right)
    theirs_out[...] = jnp.where(early, right, left)


def send_half(source, mine_out, theirs_out, place, in_first):
    mine = (lax.axis_index("section") == 0) == in_first
    for chosen, out in ((mine, mine_out), (jnp.logical_not(mine), theirs_out)):

        @pl.when(chosen)
        def _(out=out):
            pltpu.make_async_copy(source, out.target.at[:, place], out.sem).start()

        out.started = True


def norm_scale(values):
    return lax.rsqrt(jnp.mean(values * values, axis=-1, keepdims=True) + EPS)


def norm_back(values, scale, gain, grad):
    weighted = grad * gain
    coupling = jnp.mean(weighted * values, axis=-1, keepdims=True)
    return scale * weighted - values * (scale * scale * scale * coupling)


def rotate(flat, cosine, sine):
    width = flat.shape[1]
    half = HEAD_DIM // 2
    lane = lax.broadcasted_iota(jnp.int32, flat.shape, 1) % HEAD_DIM
    partner = jnp.where(
        lane < half, pltpu.roll(flat, width - half, 1), pltpu.roll(flat, half, 1)
    )
    return flat * cosine + partner * sine


def key_tables(cosine, sine):
    lane = lax.broadcasted_iota(jnp.int32, cosine.shape, 1)
    is_key = lane < cosine.shape[1] // 2
    return jnp.where(is_key, cosine, 1.0), jnp.where(is_key, sine, 0.0)


def qkv_copies(wq, wk, wv, q_buf, kv_buf, sem):
    kv = wk[0].shape[1]
    return [
        (wq[0].at[0], wq[1].at[0], q_buf, sem.at[0]),
        (wk[0].at[0], wk[1].at[0], kv_buf.at[pl.ds(0, kv)], sem.at[1]),
        (wv[0].at[0], wv[1].at[0], kv_buf.at[pl.ds(kv, kv)], sem.at[2]),
    ]


def norm_qkv(layer, first, ins, outs, *scratch):
    gain, cosine, sine = ins[:3]
    query_out, kv_out, normed_out, query_saved = outs[:4]
    copies = []
    if first:
        q_buf, kv_buf, sem = scratch
        copies = qkv_copies(ins[3:5], ins[5:7], ins[7:9], q_buf, kv_buf, sem)
        fetch(layer, copies)
        hidden = ins[9][...].astype(F32)
    else:
        q_buf, kv_buf = ins[3:5]
        low = (ins[5][...].astype(F32) + summed(ins[6:], scratch[0])).astype(BF)
        outs[4][...] = low
        outs[4].send()
        hidden = low.astype(F32)
    normed = (hidden * norm_scale(hidden) * gain[...]).astype(BF)
    normed_out[...] = normed
    normed_out.send()
    cos, sin = cosine[...], sine[...]
    key_cos, key_sin = key_tables(cos, sin)
    for own, _, buffer, one in copies:
        arrived(own, buffer, one)
    query = rotate(dot(normed, q_buf[...]), cos, sin).astype(BF)
    query_saved[...] = query
    query_saved.send()
    query_out[...] = query
    kv_out[...] = rotate(dot_t(normed, kv_buf[...]), key_cos, key_sin).astype(BF)


def split_keys(kv_refs, k_buf, v_buf):
    groups = k_buf.shape[0]
    rows = k_buf.shape[1] // len(kv_refs)
    for index, ref in enumerate(kv_refs):
        block = ref[...]
        for group in range(groups):
            low = group * HEAD_DIM
            k_buf[group, index * rows : (index + 1) * rows, :] = block[:, low : low + HEAD_DIM]
            low = (groups + group) * HEAD_DIM
            v_buf[group, index * rows : (index + 1) * rows, :] = block[:, low : low + HEAD_DIM]


def attention(ins, outs, q_buf, sum_buf):
    wo_buf, bias, query = ins[:3]
    kv_refs = ins[3:]
    mine_out, theirs_out, attn_out, lse_out, k_buf, v_buf = outs[:6]
    heads = q_buf.shape[0]
    group_size = heads // k_buf.buffer.shape[0]
    split_query(query[...], q_buf)
    split_keys(kv_refs, k_buf.buffer, v_buf.buffer)
    k_buf.send()
    v_buf.send()
    results, totals = [], []
    for head in range(heads):
        group = head // group_size
        scores = dot_t(q_buf[head], k_buf[group]) * FACTOR + bias[...]
        top = jnp.max(scores, axis=-1, keepdims=True)
        weights = jnp.exp(scores - top)
        total = jnp.sum(weights, axis=-1, keepdims=True)
        totals.append(top + jnp.log(total))
        chances = (weights * (1.0 / total)).astype(BF)
        results.append(dot(chances, v_buf[group]))
    attn = jnp.concatenate(results, axis=1)
    attn_out[...] = attn
    attn_out.send()
    lse_out[...] = jnp.concatenate(totals, axis=1)
    rows = attn.astype(BF)
    store_halves(rows, mine_out, theirs_out)
    sum_buf[...] = dot(rows, wo_buf[...])
    store_shares(sum_buf, outs[6:])


def split_query(query, q_buf):
    for head in range(q_buf.shape[0]):
        q_buf[head] = query[:, head * HEAD_DIM : (head + 1) * HEAD_DIM]


def mlp(ins, outs, total, rows_buf, act_buf):
    wg, wu, wd, hidden, gain = ins[:5]
    middle_out, normed_out, gate_out, up_out, mine_out, theirs_out = outs[:6]
    middle = hidden[...].astype(F32) + summed(ins[5:], rows_buf)
    middle_out[...] = middle.astype(BF)
    middle_out.send()
    normed_out[...] = (middle * norm_scale(middle) * gain[...]).astype(BF)
    normed_out.send()
    for step in range(wg.shape[1] // TILE):
        part = slice(step * TILE, (step + 1) * TILE)
        gate = dot(normed_out[...], wg[:, part])
        upward = dot(normed_out[...], wu[:, part])
        gate_out[:, part] = gate.astype(BF)
        up_out[:, part] = upward.astype(BF)
        act = (gate * jax.nn.sigmoid(gate) * upward).astype(BF)
        gate_out.send((slice(None), part))
        up_out.send((slice(None), part))
        act_buf[:, part] = act
        half = act_buf.shape[1] // 2
        place = slice(step * TILE % half, step * TILE % half + TILE)
        send_half(act_buf.at[:, part], mine_out, theirs_out, place, step * TILE < half)
        term = dot(act, wd[part, :])
        if step == 0:
            total[...] = term
        else:
            total[...] += term
    store_shares(total, outs[6:])


def mlp_back(last, ins, outs, total, rows_buf):
    wg, wu, wd, gate_ref, up_ref = ins[:5]
    mine_out, theirs_out = outs[:2]
    shares = outs[2:] if last else outs[2:-2]
    early = lax.axis_index("section") == 0
    if last:
        grad_ref = ins[5]
    else:
        middle_grad, hidden, gain = ins[5:8]
        grad_ref, gain_out = outs[-2:]
        values, grad = hidden[...].astype(F32), summed(ins[8:], rows_buf)
        scale = norm_scale(values)
        gain_out[...] = jnp.sum(grad * values * scale, axis=0, keepdims=True)
        grad_ref[...] = (middle_grad[...].astype(F32) + norm_back(values, scale, gain[...], grad)).astype(BF)
        grad_ref.send()
    for step in range(wg.shape[1] // TILE):
        part = slice(step * TILE, (step + 1) * TILE)
        act_grad = dot_t(grad_ref[...], wd[part, :])
        gate, upward = gate_ref[:, part].astype(F32), up_ref[:, part].astype(F32)
        sigma = jax.nn.sigmoid(gate)
        gate_grad = (act_grad * upward * sigma * (1.0 + gate * (1.0 - sigma))).astype(BF)
        up_grad = (act_grad * gate * sigma).astype(BF)
        mine_out[:, part] = jnp.where(early, gate_grad, up_grad)
        theirs_out[:, part] = jnp.where(early, up_grad, gate_grad)
        theirs_out.send((slice(None), part))
        mine_out.send((slice(None), part))
        term = dot_t(gate_grad, wg[:, part]) + dot_t(up_grad, wu[:, part])
        if step == 0:
            total[...] = term
        else:
            total[...] += term
    store_shares(total, shares)


def attention_back(peers, ins, outs, q_buf, dk_buf, dv_buf, rows_buf):
    wo_buf, grad_in, middle, gain, query, bias, attn, lse, cosine, sine, k_buf, v_buf = ins[:12]
    sums = ins[12:]
    low_out, gain_out, pre_out = outs[:3]
    block_outs = outs[3:]
    heads, groups = q_buf.shape[0], k_buf.shape[0]
    group_size = heads // groups
    grad = summed(sums, rows_buf)
    values = middle[...].astype(F32)
    scale = norm_scale(values)
    gain_out[...] = jnp.sum(grad * values * scale, axis=0, keepdims=True)
    middle_grad = grad_in[...].astype(F32) + norm_back(values, scale, gain[...], grad)
    low_out[...] = middle_grad.astype(BF)
    low_out.send()
    attn_grad = dot_t(low_out[...], wo_buf[...]).astype(BF)
    split_query(query[...], q_buf)
    query_grads = []
    for head in range(heads):
        group = head // group_size
        lanes = slice(head * HEAD_DIM, (head + 1) * HEAD_DIM)
        head_grad = attn_grad[:, lanes]
        delta = jnp.sum(head_grad.astype(F32) * attn[:, lanes], axis=-1, keepdims=True)
        scores = dot_t(q_buf[head], k_buf[group]) * FACTOR + bias[...]
        chances = jnp.exp(scores - lse[:, head : head + 1])
        chance_grad = dot_t(head_grad, v_buf[group])
        score_grad = (chances * (chance_grad - delta) * FACTOR).astype(BF)
        query_grads.append(dot(score_grad, k_buf[group]))
        key_term = outer(score_grad, q_buf[head])
        value_term = outer(chances.astype(BF), head_grad)
        if head % group_size == 0:
            dk_buf[group] = key_term
            dv_buf[group] = value_term
        else:
            dk_buf[group] += key_term
            dv_buf[group] += value_term
    rows = middle_grad.shape[0]
    for index in reversed(range(peers)):
        span = slice(index * rows, (index + 1) * rows)
        block = jnp.concatenate(
            [dk_buf[group, span, :] for group in range(groups)]
            + [dv_buf[group, span, :] for group in range(groups)],
            axis=1,
        )
        block_outs[index][...] = block if index == 0 else block.astype(BF)
        block_outs[index].send()
    query_grad = jnp.concatenate(query_grads, axis=1)
    pre_out[...] = rotate(query_grad, cosine[...], -sine[...]).astype(BF)


def qkv_back(ins, outs, total):
    q_buf, kv_buf, cosine, sine, pre_query, own = ins[:6]
    mine_out, theirs_out = outs[:2]
    both = own[...]
    for ref in ins[6:]:
        both = both + ref[...].astype(F32)
    key_cos, key_sin = key_tables(cosine[...], sine[...])
    pre = rotate(both, key_cos, -key_sin).astype(BF)
    early = lax.axis_index("section") == 0
    pre_q = pre_query[...]
    mine_out[...] = jnp.where(early, pre_q, pre)
    theirs_out[...] = jnp.where(early, pre, pre_q)
    theirs_out.send()
    mine_out.send()
    total[...] = dot_t(pre_q, q_buf[...]) + dot(pre, kv_buf[...])
    store_shares(total, outs[2:])


def last_output(ins, outs, rows_buf):
    outs[0][...] = (ins[0][...].astype(F32) + summed(ins[1:], rows_buf)).astype(BF)


def finish(ins, outs, rows_buf):
    middle_grad, hidden, gain = ins[:3]
    values, grad = hidden[...].astype(F32), summed(ins[3:], rows_buf)
    scale = norm_scale(values)
    outs[0][...] = (middle_grad[...].astype(F32) + norm_back(values, scale, gain[...], grad)).astype(BF)
    outs[0].send()
    outs[1][...] = jnp.sum(grad * values * scale, axis=0, keepdims=True)


def grad_blocks(spread, ins, outs, *scratch):
    buffer = scratch[0] if spread else outs[0].buffer
    peers = len(outs) if spread else outs[0].buffer.shape[0]
    me = lax.axis_index("dp")
    start = 0
    for left, left_other, right, right_other in zip(*[iter(ins)] * 4):
        wide, wide_other = right[...], right_other[...]
        size = left.buffer.shape[1] // peers
        lanes = slice(start, start + wide.shape[1])
        for block in range(peers):
            span = slice(block * size, (block + 1) * size)
            term = outer(left[:, span], wide) + outer(left_other[:, span], wide_other)
            place = lax.bitwise_xor(me, block) if spread else block
            buffer[place, :, lanes] = term.astype(BF)
        start += wide.shape[1]
    if start < buffer.shape[-1]:
        rest = buffer.shape[-1] - start
        buffer[:, :, start:] = jnp.zeros((peers, buffer.shape[1], rest), BF)
    if spread:
        for index, out in enumerate(outs):
            out[...] = buffer[index]
            out.send()


def add_blocks(ins, outs):
    total = ins[0][...].astype(F32)
    for block in ins[1:]:
        total = total + block[...].astype(F32)
    outs[0][...] = total.astype(BF)


def grad_parts(kept, received):
    early = lax.axis_index("section") == 0

    def halves(lanes):
        own, other = kept[:, lanes].astype(F32), received[:, lanes].astype(F32)
        return jnp.where(early, own, other), jnp.where(early, other, own)

    return halves


def mlp_grads(ins, outs):
    halves = grad_parts(*ins)
    gate_out, up_out, down_out = outs
    ff = gate_out.buffer.shape[1]
    gate, upward = halves(slice(0, ff))
    gate_out[...] = gate
    gate_out.send()
    up_out[...] = upward
    up_out.send()
    half = ff // 2
    for index, part in enumerate(halves(slice(ff, ff + half))):
        down_out[index * half : (index + 1) * half, :] = part.T


def head_grads(ins, outs):
    halves = grad_parts(*ins)
    out_out, query_out, key_out, value_out = outs
    half = out_out.buffer.shape[0] // 2
    for index, part in enumerate(halves(slice(0, half))):
        out_out[index * half : (index + 1) * half, :] = part.T
    query, key_value = halves(slice(half, 3 * half))
    query_out[...] = query
    flipped = key_value.T
    key_out[...] = flipped[:half]
    value_out[...] = flipped[half:]


def add_shares(ins, outs):
    total = ins[0][...].astype(F32)
    for ref in ins[1:]:
        total = total + ref[...].astype(F32)
    outs[0][...] = total.astype(BF)


def spread(values):
    peers = len(values)
    return [values[0]] + [
        lax.ppermute(values[step], "tensor", [(peer, peer ^ step) for peer in range(peers)])
        for step in range(1, peers)
    ]


def add_rows(received, after=()):
    (total,) = kernel_call(
        add_shares,
        "add_shares",
        near(received),
        near([shape(received[0].shape, BF)]),
        after=after,
        cost=0.5,
    )
    return total


def sum_tensor(parts):
    return spread([add_rows(spread(parts))] * len(parts))


def layout(lengths, token_count):
    seq_ends = jnp.cumsum(lengths)
    starts = seq_ends - lengths
    places = jnp.arange(token_count, dtype=jnp.int32)
    segment = jnp.sum((places[:, None] >= seq_ends[None, :]).astype(jnp.int32), axis=1)
    labels = jnp.arange(lengths.shape[0], dtype=jnp.int32)
    offset = jnp.sum(jnp.where(segment[:, None] == labels[None, :], starts[None, :], 0), axis=1)
    return (segment, places - offset)


def rope_tables(position, heads):
    halfway = HEAD_DIM // 2
    inverse = THETA ** (-2.0 * jnp.arange(halfway, dtype=F32) / HEAD_DIM)
    angles = position.astype(F32)[:, None] * inverse[None, :]
    cosine, sine = jnp.cos(angles), jnp.sin(angles)
    return (
        jnp.tile(jnp.concatenate([cosine, cosine], axis=-1), (1, heads)),
        jnp.tile(jnp.concatenate([-sine, sine], axis=-1), (1, heads)),
    )


def peer_pairs(peers, step, later):
    pairs = [(low, low ^ step) for low in range(peers) if low < low ^ step]
    return [(high, low) for low, high in pairs] if later else pairs


def per_device(
    layer_input,
    seq_lengths,
    norm1_gain,
    w_query,
    w_key,
    w_value,
    w_out,
    norm2_gain,
    w_gate,
    w_up,
    w_down,
    out_grad,
):
    Order.token, Order.pending = (), []
    rows, width = layer_input.shape[1:]
    peers = lax.axis_size("dp")
    me = lax.axis_index("dp")
    first = lax.axis_index("section") == 0
    q_width, kv_width, ff = w_query.shape[2], w_key.shape[2], w_gate.shape[2]
    heads, groups = q_width // HEAD_DIM, kv_width // HEAD_DIM
    tokens = rows * peers
    shares = lax.axis_size("tensor")

    def pick(early, late):
        return jnp.where(first, early, late)

    own = [w_query, jnp.swapaxes(w_key, 1, 2), jnp.swapaxes(w_value, 1, 2), w_out, w_gate, w_up, w_down]
    wq, wk, wv = [(weight, swap(weight)) for weight in own[:3]]
    gains = []
    for gain in (norm1_gain, norm2_gain):
        other = swap(gain)
        gains.append((pick(gain, other), pick(other, gain)))

    segment, position = layout(pick(seq_lengths[0], seq_lengths[1]), tokens)
    row_seg = lax.dynamic_slice_in_dim(segment, me * rows, rows, 0)
    row_pos = lax.dynamic_slice_in_dim(position, me * rows, rows, 0)
    local = jnp.arange(rows, dtype=jnp.int32)
    key_place = jnp.concatenate([(me ^ step) * rows + local for step in range(peers)])
    key_seg = jnp.concatenate(
        [lax.dynamic_slice_in_dim(segment, (me ^ step) * rows, rows, 0) for step in range(peers)]
    )
    allowed = (row_seg[:, None] == key_seg[None, :]) & (
        key_place[None, :] <= (me * rows + local)[:, None]
    )
    bias = jnp.where(allowed, 0.0, MASKED).astype(F32)
    cosine, sine = rope_tables(row_pos, heads)

    share = shape((rows // shares, width), BF)
    share_outs = near([share] * shares)
    rows_buf = pltpu.VMEM((rows, width), BF)
    total_buf = pltpu.VMEM((rows, width), F32)
    row_f32 = shape((rows, width), F32)
    row_bf = shape((rows, width), BF)
    line = shape((1, width), F32)
    head_bf = shape((rows, q_width), BF)
    half_head = shape((rows, q_width // 2), BF)
    half_wide = shape((rows, ff // 2), BF)
    kv_bf = shape((rows, 2 * kv_width), BF)
    wide_f32 = shape((rows, ff), F32)
    wide_bf = shape((rows, ff), BF)
    dma = pltpu.SemaphoreType.DMA
    qkv_scratch = [
        pltpu.VMEM((width, q_width), BF),
        pltpu.VMEM((2 * kv_width, width), BF),
    ]
    mlp_scratch = [total_buf, rows_buf]
    keys_bf = shape((groups, tokens, HEAD_DIM), BF)
    head_scratch = [pltpu.VMEM((heads, rows, HEAD_DIM), BF)]

    def run_qkv(layer, ins, after):
        start = layer == 0
        outs = near([head_bf, kv_bf]) + far([row_bf, head_bf])
        return kernel_call(
            functools.partial(norm_qkv, layer, start),
            f"norm_qkv_{layer}",
            ins,
            outs if start else outs + far([row_bf]),
            qkv_scratch + [dma((3,))] if start else [rows_buf],
            after,
            cost=4.0,
        )

    def run_attention(layer, brought, query, blocks, after):
        outs = [half_head] * 2 + [shape((rows, q_width), F32), shape((rows, heads), F32)] + [keys_bf] * 2
        return kernel_call(
            attention,
            f"attention_{layer}",
            brought + near([query, *blocks]),
            far(outs) + share_outs,
            head_scratch + [total_buf],
            after,
            cost=5.0,
            limit=min(8 + 4 * peers, 28),
        )

    def run_mlp(layer, brought, sums, after):
        return kernel_call(
            mlp,
            f"mlp_{layer}",
            brought + near(sums),
            far([row_bf, row_bf, wide_bf, wide_bf, half_wide, half_wide])
            + (share_outs if layer == 0 else far([share] * shares)),
            mlp_scratch + [pltpu.VMEM((rows, ff), BF)],
            after,
            cost=6.0,
            limit=24,
        )

    def run_mlp_back(layer, brought, sums, after):
        last = layer == 1
        outs = far([wide_bf, wide_bf]) + share_outs
        return kernel_call(
            functools.partial(mlp_back, last),
            f"mlp_back_{layer}",
            brought + near(sums),
            outs if last else outs + far([row_bf, line]),
            mlp_scratch,
            after,
            cost=8.0,
            limit=24,
        )

    def run_attention_back(layer, brought, sums, after):
        return kernel_call(
            functools.partial(attention_back, peers),
            f"attention_back_{layer}",
            brought + near(sums),
            far([row_bf, line, head_bf, shape((rows, 2 * kv_width), F32)] + [kv_bf] * (peers - 1)),
            head_scratch
            + [
                pltpu.VMEM((groups, tokens, HEAD_DIM), F32),
                pltpu.VMEM((groups, tokens, HEAD_DIM), F32),
                rows_buf,
            ],
            after,
            cost=9.0,
            limit=min(8 + 4 * peers, 40),
        )

    def run_qkv_back(layer, brought, pieces, after):
        return kernel_call(
            qkv_back,
            f"qkv_back_{layer}",
            brought + loose(pieces),
            far([kv_bf, kv_bf]) + share_outs,
            [total_buf],
            after,
            cost=4.0,
        )

    def weight_grad(groups, name, direct, after=()):
        ins, tall = [], 0
        for left, left_other, mine, mine_other in groups:
            ins += far([left]) + loose([left_other]) + far([mine]) + loose([mine_other])
            tall += mine.shape[1]
        if not direct:
            tall = -(-tall // 128) * 128
        block = shape((width // peers, tall), BF)
        whole = shape((peers, width // peers, tall), BF)
        blocks = kernel_call(
            functools.partial(grad_blocks, direct),
            name,
            ins,
            far([block] * peers if direct else [whole]),
            [pltpu.VMEM(whole.shape, BF)] if direct else [],
            after,
            cost=8.0,
        )
        if not direct:
            return lax.psum_scatter(blocks[0], "dp", scatter_dimension=0, tiled=False)
        pieces = [blocks[0]]
        for step in range(1, peers):
            pairing = [(peer, peer ^ step) for peer in range(peers)]
            pieces.append(lax.ppermute(blocks[step], "dp", pairing))

        def total():
            return kernel_call(
                add_blocks, "add_" + name, far(pieces[:1]) + loose(pieces[1:]), far([block])
            )[0]

        return total

    def whole_grads(body, name, per_layer, dims):
        kept = pick(per_layer[0], per_layer[1])
        received = swap(pick(per_layer[1], per_layer[0]))
        return kernel_call(
            body, name, loose([kept, received]), far([shape(dim, F32) for dim in dims]), cost=4.0
        )

    def by_layer(per_layer):
        received = swap(pick(per_layer[1], per_layer[0]))
        kept = pick(per_layer[0], per_layer[1])
        return jnp.stack([pick(kept, received), pick(received, kept)])[None]

    hidden = pick(layer_input[0], layer_input[1])
    grad = pick(out_grad[0], out_grad[1])
    saved, outputs = [], []
    for layer in range(2):
        if layer == 0:
            ins = far([gains[0][layer], cosine, sine]) + weights([wq, wk, wv]) + far([hidden])
            query, kv, normed_one, query_saved = run_qkv(layer, ins, [])
        else:
            ins = ready[2:5] + ready[:2] + ready[5:] + near(sums)
            query, kv, normed_one, query_saved, hidden = run_qkv(layer, ins, collect())
            outputs.append(hidden)
        if layer == 0:
            wo, wg = follow(own[3:5], normed_one)
        blocks = [kv]
        for step in range(1, peers):
            blocks.append(lax.ppermute(kv, "dp", peer_pairs(peers, step, False)))
        early = collect()
        if layer == 0:
            early += [(wg[1], LOOSE_RAW)]
        else:
            grad_other = soon(grad)
            early += collect()
        ready = bring(layer, f"bring_attention_{layer}", [[wo]], [bias])
        *results, attn, lse, keys, values = (outs := run_attention(layer, ready, query, blocks, early))[:-shares]
        received = spread(outs[-shares:])
        if layer == 0:
            wu, wd = follow(own[5:], results[1])
            total = add_rows(received, [(wu[1], LOOSE_RAW), (wd[1], LOOSE_RAW)])
        else:
            total = add_rows(received)
        swapped, theirs, _ = lax.optimization_barrier((normed_one, results[1], total))
        normed_one = (normed_one, soon(swapped))
        head_halves = (results[0], soon(theirs))
        sums = spread([total] * shares)
        ready = bring(layer, f"bring_mlp_{layer}", [[wg], [wu], [wd]], [hidden, gains[1][layer]])
        early = collect()
        middle, normed_two, gate, upward, act_mine, act_theirs, *parts = run_mlp(
            layer, ready, sums, early
        )
        if layer == 0:
            sums = sum_tensor(parts)
            ready = bring(
                1, "bring_qkv_1", [[wq], [wk, wv]], [gains[0][1], cosine, sine, middle]
            )
        early = collect()
        act_halves = (act_mine, soon(act_theirs))
        normed_two = (normed_two, soon(normed_two))
        Order.pending += [value for value, _ in early]
        saved.append(
            (hidden, query_saved, (keys, values), normed_one, head_halves, attn, lse)
            + (middle, normed_two, gate, upward, act_halves)
        )

    last_middle, last_parts = middle, parts
    in_grads, vectors, mlp_totals = [None, None], [None, None], [None, None]
    source, sums = [grad], []
    for layer in (1, 0):
        (hidden, query, blocks, normed_one, head_halves, attn, lse) = saved[layer][:7]
        (middle, normed_two, gate, upward, act_halves) = saved[layer][7:]
        if layer == 1:
            mine, theirs, *parts = run_mlp_back(layer, ready[:3] + far([gate, upward, grad]), [], [])
        else:
            mine, theirs, *parts, grad, gain_one = run_mlp_back(
                layer, ready + far([gate, upward, *source]), sums, []
            )
            in_grads[1] = grad
        if layer == 0:
            grad_other = soon(grad)
        mlp_groups = [(*normed_two, mine, soon(theirs)), (grad, grad_other, *act_halves)]
        received = spread(parts)
        sums = spread([add_rows(received, collect())] * shares)
        due = []
        if layer == 1:
            last_received = spread(last_parts)
        else:
            mlp_totals[0] = weight_grad(mlp_groups, "grad_mlp_0", False)
            due = []
        brought = bring(
            layer,
            f"bring_attention_back_{layer}",
            [[wo]],
            [grad, middle, gains[1][layer], query, bias, attn, lse, cosine, sine, *blocks],
        )
        low, gain_two, pre_query, *pieces = run_attention_back(layer, brought, sums, due)
        low_other = soon(low)
        far_pieces = [
            lax.ppermute(pieces[step], "dp", peer_pairs(peers, step, True))
            for step in range(1, peers)
        ]
        if layer == 1:
            last_sums = spread([add_rows(last_received)] * shares)
            mlp_totals[1] = weight_grad(
                mlp_groups, "grad_mlp_1", False, [(far_pieces[0], LOOSE_RAW)]
            )
        else:
            (output,) = kernel_call(
                last_output,
                "last_output",
                far([last_middle]) + near(last_sums),
                far([row_bf]),
                [rows_buf],
                cost=2.0,
            )
            outputs.append(output)
        ready = bring(
            layer,
            f"bring_qkv_back_{layer}",
            [[wq], [wk, wv]],
            [cosine, sine, pre_query, pieces[0]],
        )
        mine, theirs, *parts = run_qkv_back(
            layer, ready, far_pieces, collect() + (raw([mlp_totals[1], head_later]) if layer == 0 else [])
        )
        head_groups = [(low, low_other, *head_halves), (*normed_one, mine, soon(theirs))]
        received = spread(parts)
        if layer == 0:
            head_total = weight_grad(head_groups, "grad_head_0", True)
            sums = spread([add_rows(received, collect())] * shares)
            head_total = head_total()
        else:
            sums = spread([add_rows(received, collect())] * shares)
            head_later = weight_grad(head_groups, "grad_head_1", False)
            ready = bring(0, "bring_mlp_back_0", [[wg], [wu], [wd]], [])
        source = [low, hidden, gains[0][layer]]
        vectors[layer] = gain_two
    in_grads[0], last_line = kernel_call(
        finish,
        "finish",
        bring(0, "bring_finish", [], source) + near(sums),
        far([row_bf, line]),
        [rows_buf],
    )
    lines = jnp.concatenate([last_line, vectors[0], gain_one, vectors[1]], axis=0)
    for axis in ("section", "dp"):
        for bit in range((lax.axis_size(axis) - 1).bit_length()):
            pairing = [(peer, peer ^ (1 << bit)) for peer in range(lax.axis_size(axis))]
            lines = lines + lax.ppermute(lines, axis, pairing)

    activations = by_layer(outputs)
    input_grads = by_layer(in_grads)
    size = width // peers
    head_parts = [head_total, head_later[:, : head_total.shape[1]]]
    grad_gate, grad_up, grad_down = whole_grads(
        mlp_grads, "mlp_grads", mlp_totals, [(size, ff), (size, ff), (ff, size)]
    )
    grad_out, grad_query, grad_key, grad_value = whole_grads(
        head_grads,
        "head_grads",
        head_parts,
        [(q_width, size), (size, q_width), (kv_width, size), (kv_width, size)],
    )
    grad_key, grad_value = grad_key.T, grad_value.T
    lines = lax.dynamic_slice_in_dim(lines, me * size, size, 1)
    return (
        activations,
        input_grads,
        pick(lines[0], lines[2])[None],
        grad_query[None],
        grad_key[None],
        grad_value[None],
        grad_out[None],
        pick(lines[1], lines[3])[None],
        grad_gate[None],
        grad_up[None],
        grad_down[None],
    )


def solution(mesh):
    placed = (
        P(None, "dp", None),
        P(),
        P("section", None),
        P("section", None, "tensor"),
        P("section", None, "tensor"),
        P("section", None, "tensor"),
        P("section", "tensor", None),
        P("section", None),
        P("section", None, "tensor"),
        P("section", None, "tensor"),
        P("section", "tensor", None),
        P(None, "dp", None),
    )
    return jax.shard_map(
        per_device,
        mesh=mesh,
        in_specs=placed,
        out_specs=(
            P("section", None, "dp", None),
            P("section", None, "dp", None),
            P("section", "dp"),
            P("section", "dp", "tensor"),
            P("section", "dp", "tensor"),
            P("section", "dp", "tensor"),
            P("section", "tensor", "dp"),
            P("section", "dp"),
            P("section", "dp", "tensor"),
            P("section", "dp", "tensor"),
            P("section", "tensor", "dp"),
        ),
        check_vma=False,
    )
```
